256 devices in a mesh: frame: 32 (over x, z), rec: 8 (over y, core).
Axes of the slice: x: 4, y: 4, z: 8, core: 2. Of those that a mesh axis runs over, the one named last changes fastest.
Arguments:
- inputs: bfloat16 [8, 32768, 512], P('rec', 'frame'), may hold values from -6 to 6
- conv_weight: bfloat16 [5, 512, 512], replicated, may hold values from -4 to 4
- conv_bias: float32 [512], replicated, may hold values from -3 to 3
- labels: int32 [8, 32768, 512], P('rec', 'frame'), may hold values 0 or 1
- rec_span: int32 [2, 8, 32768], P(None, 'rec', 'frame'), may hold values from 0 to 1023, as said below
Outputs:
- features: bfloat16 [8, 32768, 512], P('rec', 'frame')
- probe_weights: float32 [512, 512], replicated
The draws below stay inside these ranges and needn't reach their ends.
Inputs may be any that keep to these rules, and one draw needn't show every extreme that they name: Each stream is a series of whole recordings of at most 1024 frames, the last one possibly cut by the stream's end: rec_span[0, g, t] counts the frames of t's recording before t and rec_span[1, g, t] those after t within the stream; in every stream some recording has exactly 1024 frames.
All inputs are finite; a program needn't handle non-finite values. No bound on the sum of `labels` on one device may be relied on, other than what follows from the above.
Results may differ from the reference program's by a relative error of at most 0.0035.
The reference program's roundings to bfloat16 on the way (of `joined`) count: a program that leaves them out, or rounds other values in their place, can miss the bound.
Values may be sent and summed in bfloat16 or wider, within the bound.
No kernel may reach another device: no remote copies, remote signals or barrier semaphores. Data moves between devices by JAX's collectives and lax.ppermute only.
A program may use at most 64 MiB of HBM per device.

```python
import math
import jax
import jax.numpy as jnp
from jax import lax

CIN = 512
FEAT = 512
LABELS = 512
TAPS = 5
REC_MOST = 1024
REC_MIN = 64
TIME = 32768
GROUPS = 8
FRAMES = 262144


def draw_rec_span(key, part):
    record_count = TIME // REC_MIN + 1
    stream_keys = jax.random.split(key, GROUPS)

    def one_stream(stream_key):
        length_key, pick_key = jax.random.split(stream_key)
        lengths = jax.random.randint(length_key, (record_count,), REC_MIN, REC_MOST + 1).astype(jnp.int32)
        longest = jax.random.randint(pick_key, (), 0, max(TIME // REC_MOST - 1, 1)).astype(jnp.int32)
        lengths = jnp.where(jnp.arange(record_count, dtype=jnp.int32) == longest, REC_MOST, lengths).astype(jnp.int32)
        record_ends = jnp.cumsum(lengths).astype(jnp.int32)
        record_starts = record_ends - lengths
        position = jnp.arange(TIME, dtype=jnp.int32)
        record_index = jnp.searchsorted(record_ends, position, side='right').astype(jnp.int32)
        before = position - record_starts[record_index]
        frames_after = jnp.minimum(record_ends[record_index], TIME) - 1 - position
        return jnp.stack([before, frames_after]).astype(jnp.int32)
    stream_spans = jax.vmap(one_stream)(stream_keys)
    return jnp.transpose(stream_spans, (1, 0, 2)).astype(jnp.int32)


def draw_conv_weight(key, part):
    base_key = jax.random.fold_in(key, 11)
    delta_key = jax.random.fold_in(key, 12)
    spread_key = jax.random.fold_in(key, 13)
    order_key = jax.random.fold_in(key, 14)
    family_count = FEAT // 4
    base = jnp.clip(jax.random.normal(base_key, (TAPS, CIN, family_count), jnp.float32), -3.0, 3.0)
    delta = jnp.clip(jax.random.normal(delta_key, (TAPS, CIN, FEAT), jnp.float32), -3.0, 3.0)
    spread = jnp.exp(jax.random.uniform(spread_key, (FEAT,), jnp.float32, math.log(0.02), 0.0))
    family = (jax.random.permutation(order_key, FEAT).astype(jnp.int32) // 4).astype(jnp.int32)
    picked = jnp.take(base, family, axis=2)
    weight = 6.0 / math.sqrt(TAPS * CIN) * (picked + spread[None, None, :] * delta)
    return weight.astype(jnp.float32).astype(jnp.bfloat16)


def plant(drawn, key, smallest, top_value):
    longest = drawn.shape.index(max(drawn.shape))
    spots = []
    for shift in (0, 1):
        where = [jax.random.randint(jax.random.fold_in(key, axis), (), 0, length) for axis, length in enumerate(drawn.shape)]
        where[longest] = (where[longest] + shift) % drawn.shape[longest]
        spots.append(tuple(where))
    return drawn.at[spots[0]].set(smallest).at[spots[1]].set(top_value)


def block_levels(rng, shape, cuts, low, high):
    def one(dim, blocks):
        draws = jax.random.uniform(jax.random.fold_in(jax.random.fold_in(rng, 6), dim), (blocks,), jnp.float32, low / len(cuts), high / len(cuts))
        return jnp.repeat(jnp.exp(draws), shape[dim] // blocks).reshape((-1,) + (1,) * (len(shape) - dim - 1))

    level = one(*cuts[0])
    for cut in cuts[1:]:
        level = level * one(*cut)
    return level


def noise(rng, extent, deviation, reach, cuts=(), kind=jnp.bfloat16):
    array = deviation * jax.random.normal(rng, extent, jnp.float32)
    if cuts:
        array = array * block_levels(rng, extent, cuts, -0.22, 0.18)
    return jnp.clip(array, -reach, reach).astype(kind)


def setup_inputs(seed: int = 0) -> dict:
    keys = jax.random.split(jax.random.key(seed), 6)
    return {
        "inputs": noise(keys[0], (GROUPS, TIME, CIN), 1.0, 6.0, ((0, 8), (1, 32))),
        "conv_weight": draw_conv_weight(jax.random.fold_in(keys[5], 71), 0),
        "conv_bias": noise(keys[2], (FEAT,), 0.5, 3.0, (), jnp.float32),
        "labels": plant((jax.random.randint(keys[3], (GROUPS, TIME, LABELS), 0, 4) < 1).astype(jnp.int32), jax.random.fold_in(keys[3], 1), 0, 1),
        "rec_span": draw_rec_span(jax.random.fold_in(keys[5], 71), 0),
    }


RIDGE = 0.1

def stack_taps(stream, before, frames_after):
    half_width = TAPS // 2
    shard_rows = stream.shape[0]
    padded = jnp.pad(stream, ((half_width, half_width), (0, 0)))
    pieces = []
    for tap_index in range(TAPS):
        offset = tap_index - half_width
        shifted = padded[tap_index:tap_index + shard_rows]
        if offset < 0:
            keep_mask = before >= -offset
        elif offset > 0:
            keep_mask = frames_after >= offset
        else:
            keep_mask = before >= 0
        pieces.append(jnp.where(keep_mask[:, None], shifted, jnp.zeros_like(shifted)))
    return jnp.concatenate(pieces, axis=1)

def reference(inputs, conv_weight, conv_bias, labels, rec_span):
    flat_weight = conv_weight.reshape(TAPS * CIN, FEAT)

    def one_group(packed):
        stream, label_rows, before, frames_after = packed
        stacked = stack_taps(stream, before, frames_after)
        pre_act = jnp.dot(stacked.astype(jnp.float32), flat_weight.astype(jnp.float32), preferred_element_type=jnp.float32) + conv_bias
        group_feats = jax.nn.gelu(pre_act, approximate=False).astype(jnp.bfloat16)
        joined = jnp.concatenate([group_feats, label_rows.astype(jnp.bfloat16)], axis=1)
        moments = jnp.dot(group_feats.T.astype(jnp.float32), joined.astype(jnp.float32), preferred_element_type=jnp.float32)
        totals = lax.optimization_barrier(jnp.sum(joined.astype(jnp.float32), axis=0))
        return (group_feats, moments, totals)
    features, moments, totals = lax.map(one_group, (inputs, labels, rec_span[0], rec_span[1]))
    moments = lax.optimization_barrier(jnp.sum(moments, axis=0))
    totals = lax.optimization_barrier(jnp.sum(totals, axis=0))
    frame_count = jnp.float32(FRAMES)
    feat_totals = totals[:FEAT]
    label_totals = totals[FEAT:]
    covariance = (moments[:, :FEAT] - feat_totals[:, None] * feat_totals[None, :] / frame_count) / frame_count
    covariance = covariance + RIDGE * jnp.eye(FEAT, dtype=jnp.float32)
    cross_terms = (moments[:, FEAT:] - feat_totals[:, None] * label_totals[None, :] / frame_count) / jnp.sqrt(frame_count)
    factor = jnp.linalg.cholesky(covariance)
    probe_weights = jax.scipy.linalg.cho_solve((factor, True), cross_terms)
    return (features, probe_weights)
```

```python
import jax
import jax.numpy as jnp
from jax import lax
from jax.sharding import Mesh, PartitionSpec as P

RIDGE = 0.1
BLOCK = 128


def frame_halo(rows, width):
    size = lax.axis_size(("x", "z"))
    up = [(i, i + 1) for i in range(size - 1)]
    down = [(j, i) for i, j in up]
    before = lax.ppermute(rows[-width:], ("x", "z"), up)
    after = lax.ppermute(rows[:width], ("x", "z"), down)
    return before, after


def all_sum(halves):
    core = lax.axis_index("core")
    swap = [(0, 1), (1, 0)]
    keep = jnp.where(core == 0, halves[0], halves[1])
    send = jnp.where(core == 0, halves[1], halves[0])
    part = keep + lax.ppermute(send, "core", swap)
    peers = lax.axis_size(("x", "y"))
    rows = part.shape[0] // peers
    chunks = lax.all_to_all(
        part.reshape(peers, rows, BLOCK), ("x", "y"), split_axis=0, concat_axis=0, tiled=True
    )
    chunk = jnp.sum(chunks, axis=0)
    for bit in (1, 2, 4):
        chunk = chunk + lax.ppermute(
            chunk, "z", [(i, i ^ bit) for i in range(lax.axis_size("z"))]
        )
    spread = jnp.broadcast_to(chunk[None], (peers, rows, BLOCK))
    full = lax.all_to_all(spread, ("x", "y"), split_axis=0, concat_axis=0, tiled=True)
    mine = full.reshape(peers * rows, BLOCK)
    other = lax.ppermute(mine, "core", swap)
    return jnp.where(core == 0, mine, other), jnp.where(core == 0, other, mine)


def per_device(inputs, conv_weight, conv_bias, labels, rec_span):
    tap_count = conv_weight.shape[0]
    half_width = tap_count // 2
    shard_rows = inputs.shape[1]
    feat_width = conv_weight.shape[2]
    label_width = labels.shape[2]
    frames_before, frames_after = frame_halo(inputs[0], half_width)
    padded = jnp.concatenate([frames_before, inputs[0], frames_after], axis=0)
    before = rec_span[0, 0]
    after = rec_span[1, 0]
    pieces = []
    for tap_index in range(tap_count):
        offset = tap_index - half_width
        shifted = padded[tap_index : tap_index + shard_rows]
        if offset < 0:
            shifted = jnp.where((before >= -offset)[:, None], shifted, jnp.zeros_like(shifted))
        elif offset > 0:
            shifted = jnp.where((after >= offset)[:, None], shifted, jnp.zeros_like(shifted))
        pieces.append(shifted)
    stacked = jnp.concatenate(pieces, axis=1)
    flat_weight = conv_weight.reshape(tap_count * conv_weight.shape[1], feat_width)
    pre_act = jnp.dot(stacked, flat_weight, preferred_element_type=jnp.float32) + conv_bias
    features = jax.nn.gelu(pre_act, approximate=False).astype(jnp.bfloat16)
    joined = jnp.concatenate([features, labels[0].astype(jnp.bfloat16)], axis=1)
    moments = lax.dot_general(
        features, joined, (((0,), (0,)), ((), ())), preferred_element_type=jnp.float32
    )
    totals = jnp.sum(joined, axis=0, dtype=jnp.float32)

    row_blocks = feat_width // BLOCK
    col_blocks = row_blocks + label_width // BLOCK
    kept = [(i, j) for i in range(row_blocks) for j in range(i, col_blocks)]
    blocks = [
        moments[i * BLOCK : (i + 1) * BLOCK, j * BLOCK : (j + 1) * BLOCK] for i, j in kept
    ]
    total_rows = totals.reshape(-1, BLOCK)
    blocks.append(jnp.pad(total_rows, ((0, BLOCK - total_rows.shape[0]), (0, 0))))
    if len(blocks) % 2:
        blocks.append(jnp.zeros((BLOCK, BLOCK), jnp.float32))
    payload = jnp.concatenate(blocks, axis=0).reshape(2, -1, BLOCK)
    first, second = all_sum(payload)
    summed = jnp.concatenate([first, second], axis=0).reshape(-1, BLOCK, BLOCK)
    place = {pair: n for n, pair in enumerate(kept)}
    totals = summed[len(kept)][: total_rows.shape[0]].reshape(-1)
    gram_block = jnp.concatenate(
        [
            jnp.concatenate(
                [
                    summed[place[i, j]] if i <= j else summed[place[j, i]].T
                    for j in range(row_blocks)
                ],
                axis=1,
            )
            for i in range(row_blocks)
        ],
        axis=0,
    )
    label_block = jnp.concatenate(
        [
            jnp.concatenate([summed[place[i, j]] for j in range(row_blocks, col_blocks)], axis=1)
            for i in range(row_blocks)
        ],
        axis=0,
    )
    frame_count = jnp.float32(
        lax.axis_size(("x", "z", "y", "core")) * inputs.shape[0] * shard_rows
    )
    feat_totals = totals[:feat_width]
    label_totals = totals[feat_width:]
    covariance = (
        gram_block - feat_totals[:, None] * feat_totals[None, :] / frame_count
    ) / frame_count
    covariance = covariance + RIDGE * jnp.eye(feat_width, dtype=jnp.float32)
    cross_terms = (
        label_block - feat_totals[:, None] * label_totals[None, :] / frame_count
    ) / jnp.sqrt(frame_count)
    factor = jnp.linalg.cholesky(covariance)
    probe_weights = jax.scipy.linalg.cho_solve((factor, True), cross_terms)
    return (features[None], probe_weights)


def solution(mesh):
    physical = Mesh(mesh.devices.reshape(4, 8, 4, 2), ("x", "z", "y", "core"))
    frame, rec = ("x", "z"), ("y", "core")
    in_specs = (P(rec, frame, None), P(), P(), P(rec, frame, None), P(None, rec, frame))
    out_specs = (P(rec, frame, None), P())
    return jax.shard_map(
        per_device, mesh=physical, in_specs=in_specs, out_specs=out_specs, check_vma=False
    )
```

```python
import functools
import math

import jax
import jax.numpy as jnp
from jax import lax
from jax.experimental import pallas as pl
from jax.experimental.pallas import tpu as pltpu
from jax.sharding import Mesh, PartitionSpec as P

RIDGE = 0.1
BLOCK = 128
GROUP = 8


def frame_halo(rows, width):
    size = lax.axis_size(("x", "z"))
    up = [(i, i + 1) for i in range(size - 1)]
    down = [(j, i) for i, j in up]
    before = lax.ppermute(rows[-width:], ("x", "z"), up)
    after = lax.ppermute(rows[:width], ("x", "z"), down)
    return before, after


def all_sum(halves):
    core = lax.axis_index("core")
    swap = [(0, 1), (1, 0)]
    keep = jnp.where(core == 0, halves[0], halves[1])
    send = jnp.where(core == 0, halves[1], halves[0])
    part = keep + lax.ppermute(send, "core", swap)
    peers = lax.axis_size(("x", "y"))
    rows = part.shape[0] // peers
    chunks = lax.all_to_all(
        part.reshape(peers, rows, BLOCK), ("x", "y"), split_axis=0, concat_axis=0, tiled=True
    )
    chunk = jnp.sum(chunks, axis=0)
    for bit in (1, 2, 4):
        chunk = chunk + lax.ppermute(
            chunk, "z", [(i, i ^ bit) for i in range(lax.axis_size("z"))]
        )
    spread = jnp.broadcast_to(chunk[None], (peers, rows, BLOCK))
    full = lax.all_to_all(spread, ("x", "y"), split_axis=0, concat_axis=0, tiled=True)
    mine = full.reshape(peers * rows, BLOCK)
    other = lax.ppermute(mine, "core", swap)
    return mine, other


def group_inverse(diag, rows):
    size = len(rows)
    for j in range(0, size, 2):
        a, b, c = diag[j][j], diag[j][j + 1], diag[j + 1][j + 1]
        scale = 1.0 / (a * c - b * b)
        left = [diag[i][j] for i in range(size)]
        right = [diag[i][j + 1] for i in range(size)]

        def solved(upper, lower):
            return (c * upper - b * lower) * scale, (a * lower - b * upper) * scale

        new = {k: solved(diag[j][k], diag[j + 1][k]) for k in range(j + 2, size)}
        for i in range(size):
            if i in (j, j + 1):
                continue
            for k in range(max(j + 2, i) if i > j else j + 2, size):
                diag[i][k] = diag[i][k] - left[i] * new[k][0] - right[i] * new[k][1]
                if i > j:
                    diag[k][i] = diag[i][k]
        for k in range(j + 2, size):
            diag[j][k], diag[j + 1][k] = new[k]
        rows[j], rows[j + 1] = solved(rows[j], rows[j + 1])
        for i in range(size):
            if i not in (j, j + 1):
                rows[i] = rows[i] - left[i] * rows[j] - right[i] * rows[j + 1]
    return rows


def spd_inverse(block):
    groups = BLOCK // GROUP
    tile = (GROUP, BLOCK)
    lane = lax.broadcasted_iota(jnp.int32, tile, 1)
    sublane = lax.broadcasted_iota(jnp.int32, tile, 0)
    part = [block[h * GROUP : (h + 1) * GROUP] for h in range(groups)]

    def spread(value):
        return jnp.broadcast_to(value, tile)

    def columns(h, first):
        return [spread(part[h][:, first + j : first + j + 1]) for j in range(GROUP)]

    def pivots(g):
        first = g * GROUP
        inside = (lane >= first) & (lane < first + GROUP)
        cols = columns(g, first)
        diag = [[None] * GROUP for _ in range(GROUP)]
        for i in range(GROUP):
            for j in range(i, GROUP):
                diag[i][j] = diag[j][i] = spread(cols[i][j : j + 1])
        rows = [
            jnp.where(
                lane == first + i, 1.0, jnp.where(inside, 0.0, spread(part[g][i : i + 1]))
            )
            for i in range(GROUP)
        ]
        return inside, diag, rows

    ahead = pivots(0)
    for g in range(groups):
        inside, diag, rows = ahead
        others = [(g + n) % groups for n in range(1, groups)]
        cols = {h: columns(h, g * GROUP) for h in others}
        rows = group_inverse(diag, rows)

        def eliminate(h):
            terms = [cols[h][j] * rows[j] for j in range(GROUP)]
            while len(terms) > 1:
                terms = [terms[n] + terms[n + 1] for n in range(0, len(terms), 2)]
            part[h] = jnp.where(inside, 0.0, part[h]) - terms[0]

        eliminate(others[0])
        if g + 1 < groups:
            ahead = pivots(g + 1)
        for h in others[1:]:
            eliminate(h)
        for i in range(GROUP):
            part[g] = jnp.where(sublane == i, rows[i], part[g])
    return jnp.concatenate(part, axis=0)


def dot32(a, b):
    return jnp.dot(a, b, precision=lax.Precision.HIGHEST, preferred_element_type=jnp.float32)


def solve_kernel(kept, row_blocks, col_blocks, frame_count, core_ref, mine_ref, other_ref, out_ref, work):
    core = core_ref[0]
    half = mine_ref.shape[0] // BLOCK

    def summed(n):
        owner, place = divmod(n, half)
        at = pl.ds(place * BLOCK, BLOCK)
        return jnp.where(core == owner, mine_ref[at, :], other_ref[at, :])

    def span(i, j=None):
        return slice(i * BLOCK, (i + 1 if j is None else j) * BLOCK)

    totals = summed(len(kept))[:col_blocks]
    diagonal = lax.broadcasted_iota(jnp.int32, (BLOCK, BLOCK), 0) == lax.broadcasted_iota(
        jnp.int32, (BLOCK, BLOCK), 1
    )
    across = [jnp.broadcast_to(totals[j : j + 1], (BLOCK, BLOCK)) for j in range(col_blocks)]
    down = [across[i].T for i in range(row_blocks)]
    for n, (i, j) in enumerate(kept):
        centred = summed(n) - down[i] * across[j] / frame_count
        if j >= row_blocks:
            work[span(i), span(j)] = centred / math.sqrt(frame_count)
        else:
            block = centred / frame_count
            work[span(i), span(j)] = jnp.where(diagonal, block + RIDGE, block) if i == j else block

    for k in range(row_blocks):
        rest = span(k + 1, col_blocks)
        inverse = spd_inverse(work[span(k), span(k)])
        flipped = {i: work[span(k), span(i)].T for i in range(k + 1, row_blocks)}
        solved = dot32(inverse, work[span(k), rest])
        work[span(k), rest] = solved
        for i in range(k + 1, row_blocks):
            at = span(i, col_blocks)
            work[span(i), at] -= dot32(flipped[i], solved[:, (i - k - 1) * BLOCK :])
        if k:
            work[span(0, k), rest] -= dot32(work[span(0, k), span(k)], solved)
    out_ref[...] = work[:, span(row_blocks, col_blocks)]


def ridge_solve(mine, other, kept, row_blocks, col_blocks, frame_count):
    core = lax.axis_index("core").astype(jnp.int32)[None]
    return pl.pallas_call(
        functools.partial(solve_kernel, kept, row_blocks, col_blocks, float(frame_count)),
        out_shape=jax.ShapeDtypeStruct(
            (row_blocks * BLOCK, (col_blocks - row_blocks) * BLOCK), jnp.float32
        ),
        in_specs=[
            pl.BlockSpec(memory_space=pltpu.SMEM),
            pl.BlockSpec(memory_space=pltpu.VMEM),
            pl.BlockSpec(memory_space=pltpu.VMEM),
        ],
        out_specs=pl.BlockSpec(memory_space=pltpu.VMEM),
        scratch_shapes=[pltpu.VMEM((row_blocks * BLOCK, col_blocks * BLOCK), jnp.float32)],
        compiler_params=pltpu.CompilerParams(vmem_limit_bytes=40 * 1024 * 1024),
        name="ridge_solve",
    )(core, mine, other)


def per_device(inputs, conv_weight, conv_bias, labels, rec_span):
    tap_count = conv_weight.shape[0]
    half_width = tap_count // 2
    shard_rows = inputs.shape[1]
    feat_width = conv_weight.shape[2]
    label_width = labels.shape[2]
    frames_before, frames_after = frame_halo(inputs[0], half_width)
    padded = jnp.concatenate([frames_before, inputs[0], frames_after], axis=0)
    before = rec_span[0, 0]
    after = rec_span[1, 0]
    pieces = []
    for tap_index in range(tap_count):
        offset = tap_index - half_width
        shifted = padded[tap_index : tap_index + shard_rows]
        if offset < 0:
            shifted = jnp.where((before >= -offset)[:, None], shifted, jnp.zeros_like(shifted))
        elif offset > 0:
            shifted = jnp.where((after >= offset)[:, None], shifted, jnp.zeros_like(shifted))
        pieces.append(shifted)
    stacked = jnp.concatenate(pieces, axis=1)
    flat_weight = conv_weight.reshape(tap_count * conv_weight.shape[1], feat_width)
    pre_act = jnp.dot(stacked, flat_weight, preferred_element_type=jnp.float32) + conv_bias
    features = jax.nn.gelu(pre_act, approximate=False).astype(jnp.bfloat16)
    joined = jnp.concatenate([features, labels[0].astype(jnp.bfloat16)], axis=1)
    moments = lax.dot_general(
        features, joined, (((0,), (0,)), ((), ())), preferred_element_type=jnp.float32
    )
    totals = jnp.sum(joined, axis=0, dtype=jnp.float32)

    row_blocks = feat_width // BLOCK
    col_blocks = row_blocks + label_width // BLOCK
    kept = [(i, j) for i in range(row_blocks) for j in range(i, col_blocks)]
    blocks = [
        moments[i * BLOCK : (i + 1) * BLOCK, j * BLOCK : (j + 1) * BLOCK] for i, j in kept
    ]
    total_rows = totals.reshape(-1, BLOCK)
    blocks.append(jnp.pad(total_rows, ((0, BLOCK - total_rows.shape[0]), (0, 0))))
    if len(blocks) % 2:
        blocks.append(jnp.zeros((BLOCK, BLOCK), jnp.float32))
    payload = jnp.concatenate(blocks, axis=0).reshape(2, -1, BLOCK)
    mine, other = all_sum(payload)
    frame_count = lax.axis_size(("x", "z", "y", "core")) * inputs.shape[0] * shard_rows
    probe_weights = ridge_solve(mine, other, kept, row_blocks, col_blocks, frame_count)
    return (features[None], probe_weights)


def solution(mesh):
    physical = Mesh(mesh.devices.reshape(4, 8, 4, 2), ("x", "z", "y", "core"))
    frame, rec = ("x", "z"), ("y", "core")
    in_specs = (P(rec, frame, None), P(), P(), P(rec, frame, None), P(None, rec, frame))
    out_specs = (P(rec, frame, None), P())
    return jax.shard_map(
        per_device, mesh=physical, in_specs=in_specs, out_specs=out_specs, check_vma=False
    )
```

```python
import functools
import math

import jax
import jax.numpy as jnp
from jax import lax
from jax.experimental import pallas as pl
from jax.experimental.pallas import tpu as pltpu
from jax.sharding import Mesh, PartitionSpec as P

RIDGE = 0.1
BLOCK = 128
GROUP = 8
TAP_REACH = 2
PAD = 8
EDGE = 16
ROWS = 256
VMEM = 56 * 1024 * 1024


def frame_halo(rows, width):
    size = lax.axis_size(("x", "z"))
    up = [(i, i + 1) for i in range(size - 1)]
    down = [(j, i) for i, j in up]
    before = lax.ppermute(rows[-width:], ("x", "z"), up)
    after = lax.ppermute(rows[:width], ("x", "z"), down)
    return before, after


def all_sum(keep, send):
    swap = [(0, 1), (1, 0)]
    part = keep + lax.ppermute(send, "core", swap)
    peers = lax.axis_size(("x", "y"))
    rows = part.shape[0] // peers
    chunks = lax.all_to_all(
        part.reshape(peers, rows, BLOCK), ("x", "y"), split_axis=0, concat_axis=0, tiled=True
    )
    chunk = jnp.sum(chunks, axis=0)
    for bit in (1, 2, 4):
        chunk = chunk + lax.ppermute(
            chunk, "z", [(i, i ^ bit) for i in range(lax.axis_size("z"))]
        )
    spread = jnp.broadcast_to(chunk[None], (peers, rows, BLOCK))
    full = lax.all_to_all(spread, ("x", "y"), split_axis=0, concat_axis=0, tiled=True)
    mine = full.reshape(peers * rows, BLOCK)
    other = lax.ppermute(mine, "core", swap)
    return mine, other


def gelu(value):
    return 0.5 * value * (1.0 + lax.erf(value * math.sqrt(0.5)))


def frames_code(span):
    before = jnp.minimum(span[0], TAP_REACH)
    after = jnp.minimum(span[1], TAP_REACH)
    return (before + (TAP_REACH + 1) * after).astype(jnp.float32)


def tap_masks(code, width):
    code = jnp.concatenate([code] * (width // BLOCK), axis=1)
    after = jnp.floor(code * (1.0 / (TAP_REACH + 1)) + 0.01)
    before = code - (TAP_REACH + 1) * after
    masks = {0: None}
    for far in range(1, TAP_REACH + 1):
        masks[-far] = before >= far - 0.5
        masks[far] = after >= far - 0.5
    return masks


def down_lanes(code_row):
    return jnp.broadcast_to(code_row, (BLOCK, BLOCK)).T


def features_of(taps_ref, rows, weight_ref, bias_ref):
    pre_act = jnp.dot(taps_ref[rows, :], weight_ref[...], preferred_element_type=jnp.float32)
    return gelu(pre_act + bias_ref[...]).astype(jnp.bfloat16)


def conv_kernel(inputs_ref, weight_ref, bias_ref, labels_ref, code_ref, joined_ref, wide, taps):
    frames, width = inputs_ref.shape
    feats = weight_ref.shape[1]
    wide[0:PAD, :] = jnp.zeros((PAD, width), jnp.float32)
    wide[PAD + frames :, :] = jnp.zeros((PAD, width), jnp.float32)
    wide[PAD : PAD + frames, :] = inputs_ref[...].astype(jnp.float32)
    for first in range(0, frames, ROWS):
        for start in range(first, first + ROWS, BLOCK):
            at = slice(start, start + BLOCK)
            masks = tap_masks(down_lanes(code_ref[start // BLOCK : start // BLOCK + 1, :]), width)
            for tap, offset in enumerate(range(-TAP_REACH, TAP_REACH + 1)):
                columns = slice(tap * width, (tap + 1) * width)
                if offset == 0:
                    taps[at, columns] = inputs_ref[at, :]
                else:
                    shifted = wide[PAD + start + offset : PAD + start + offset + BLOCK, :]
                    taps[at, columns] = jnp.where(masks[offset], shifted, 0.0).astype(jnp.bfloat16)
        rows = slice(first, first + ROWS)
        joined_ref[rows, feats:] = labels_ref[rows, :].astype(jnp.float32).astype(jnp.bfloat16)
        joined_ref[rows, :feats] = features_of(taps, rows, weight_ref, bias_ref)


def moments_kernel(
    kept, core_ref, joined_ref, inputs_ref, halo_ref, weight_ref, bias_ref, code_ref,
    features_ref, keep_ref, send_ref, joined, edges, taps, blocks, sems,
):
    frames, width = inputs_ref.shape
    feats = weight_ref.shape[1]
    last = frames - EDGE
    edges[0, 0:PAD, :] = jnp.concatenate(
        [jnp.zeros((PAD - TAP_REACH, width), jnp.float32), halo_ref[0:TAP_REACH, :].astype(jnp.float32)], axis=0
    )
    edges[0, PAD:, :] = inputs_ref[0 : EDGE + PAD, :].astype(jnp.float32)
    edges[1, 0 : EDGE + PAD, :] = inputs_ref[last - PAD :, :].astype(jnp.float32)
    edges[1, EDGE + PAD :, :] = jnp.concatenate(
        [halo_ref[TAP_REACH:, :].astype(jnp.float32), jnp.zeros((PAD - TAP_REACH, width), jnp.float32)], axis=0
    )
    for side, first in enumerate((0, last)):
        block = first // BLOCK
        code = down_lanes(code_ref[block : block + 1, :])[first % BLOCK : first % BLOCK + EDGE]
        masks = tap_masks(code, width)
        at = slice(side * EDGE, (side + 1) * EDGE)
        for tap, offset in enumerate(range(-TAP_REACH, TAP_REACH + 1)):
            shifted = edges[side, PAD + offset : PAD + offset + EDGE, :]
            if offset:
                shifted = jnp.where(masks[offset], shifted, 0.0)
            taps[at, tap * width : (tap + 1) * width] = shifted.astype(jnp.bfloat16)
    joined[...] = joined_ref[...]
    edge_features = features_of(taps, slice(None), weight_ref, bias_ref)
    joined[0:EDGE, :feats] = edge_features[:EDGE]
    joined[last:, :feats] = edge_features[EDGE:]
    features_ref[...] = joined[:, :feats]

    totals = jnp.dot(
        jnp.ones((16, frames), jnp.bfloat16), joined[...], preferred_element_type=jnp.float32
    )[0:1]
    row_blocks = feats // BLOCK
    lane = lax.broadcasted_iota(jnp.int32, (8, BLOCK), 1)
    zero_rows = jnp.zeros((4, BLOCK), jnp.float32)
    half = blocks.shape[1] // BLOCK
    places = {pair: divmod(n, half) for n, pair in enumerate(kept)}
    for first in range(0, row_blocks, 2):
        left = joined[:, first * BLOCK : (first + 2) * BLOCK]
        right = joined[:, first * BLOCK :]
        moments = lax.dot_general(
            left, right, (((0,), (0,)), ((), ())), preferred_element_type=jnp.float32
        )
        for i in (first, first + 1):
            for j in range(i, joined.shape[1] // BLOCK):
                owner, place = places[i, j]
                block = moments[
                    (i - first) * BLOCK : (i - first + 1) * BLOCK,
                    (j - first) * BLOCK : (j - first + 1) * BLOCK,
                ]
                blocks[owner, place * BLOCK : (place + 1) * BLOCK, :] = block
                if i == j:
                    pair = [totals[:, n * BLOCK : (n + 1) * BLOCK] for n in (i, i + row_blocks)]
                    rows = [row for t in pair for row in (t, pltpu.roll(t, BLOCK // 2, 1))]
                    middle = BLOCK // 2
                    spot = slice(place * BLOCK + middle, place * BLOCK + middle + 8)
                    blocks[owner, spot, :] = jnp.where(
                        lane < middle, jnp.concatenate(rows + [zero_rows], axis=0), block[middle : middle + 8]
                    )
    core = core_ref[0]
    copies = [
        pltpu.make_async_copy(blocks.at[core], keep_ref, sems.at[0]),
        pltpu.make_async_copy(blocks.at[1 - core], send_ref, sems.at[1]),
    ]
    for copy in copies:
        copy.start()
    for copy in copies:
        copy.wait()


def group_inverse(diag, rows):
    size = len(rows)
    for j in range(0, size, 2):
        a, b, c = diag[j][j], diag[j][j + 1], diag[j + 1][j + 1]
        scale = 1.0 / (a * c - b * b)
        left = [diag[i][j] for i in range(size)]
        right = [diag[i][j + 1] for i in range(size)]

        def solved(upper, lower):
            return (c * upper - b * lower) * scale, (a * lower - b * upper) * scale

        new = {k: solved(diag[j][k], diag[j + 1][k]) for k in range(j + 2, size)}
        for i in range(size):
            if i in (j, j + 1):
                continue
            for k in range(max(j + 2, i) if i > j else j + 2, size):
                diag[i][k] = diag[i][k] - left[i] * new[k][0] - right[i] * new[k][1]
                if i > j:
                    diag[k][i] = diag[i][k]
        for k in range(j + 2, size):
            diag[j][k], diag[j + 1][k] = new[k]
        rows[j], rows[j + 1] = solved(rows[j], rows[j + 1])
        for i in range(size):
            if i not in (j, j + 1):
                rows[i] = rows[i] - left[i] * rows[j] - right[i] * rows[j + 1]
    return rows


def spd_inverse(block):
    groups = BLOCK // GROUP
    tile = (GROUP, BLOCK)
    lane = lax.broadcasted_iota(jnp.int32, tile, 1)
    sublane = lax.broadcasted_iota(jnp.int32, tile, 0)
    part = [block[h * GROUP : (h + 1) * GROUP] for h in range(groups)]

    def spread(value):
        return jnp.broadcast_to(value, tile)

    def columns(h, first):
        return [spread(part[h][:, first + j : first + j + 1]) for j in range(GROUP)]

    def pivots(g):
        first = g * GROUP
        inside = (lane >= first) & (lane < first + GROUP)
        cols = columns(g, first)
        diag = [[None] * GROUP for _ in range(GROUP)]
        for i in range(GROUP):
            for j in range(i, GROUP):
                diag[i][j] = diag[j][i] = spread(cols[i][j : j + 1])
        rows = [
            jnp.where(
                lane == first + i, 1.0, jnp.where(inside, 0.0, spread(part[g][i : i + 1]))
            )
            for i in range(GROUP)
        ]
        return inside, diag, rows

    ahead = pivots(0)
    for g in range(groups):
        inside, diag, rows = ahead
        others = [(g + n) % groups for n in range(1, groups)]
        cols = {h: columns(h, g * GROUP) for h in others}
        rows = group_inverse(diag, rows)

        def eliminate(h):
            terms = [cols[h][j] * rows[j] for j in range(GROUP)]
            while len(terms) > 1:
                terms = [terms[n] + terms[n + 1] for n in range(0, len(terms), 2)]
            part[h] = jnp.where(inside, 0.0, part[h]) - terms[0]

        eliminate(others[0])
        if g + 1 < groups:
            ahead = pivots(g + 1)
        for h in others[1:]:
            eliminate(h)
        for i in range(GROUP):
            part[g] = jnp.where(sublane == i, rows[i], part[g])
    return jnp.concatenate(part, axis=0)


def dot32(a, b):
    return jnp.dot(a, b, precision=lax.Precision.HIGHEST, preferred_element_type=jnp.float32)


def solve_kernel(kept, row_blocks, col_blocks, frame_count, core_ref, mine_ref, other_ref, out_ref, work):
    core = core_ref[0]
    half = mine_ref.shape[0] // BLOCK

    def summed(n):
        owner, place = divmod(n, half)
        at = pl.ds(place * BLOCK, BLOCK)
        return jnp.where(core == owner, mine_ref[at, :], other_ref[at, :])

    def span(i, j=None):
        return slice(i * BLOCK, (i + 1 if j is None else j) * BLOCK)

    diagonal = lax.broadcasted_iota(jnp.int32, (BLOCK, BLOCK), 0) == lax.broadcasted_iota(
        jnp.int32, (BLOCK, BLOCK), 1
    )
    middle = BLOCK // 2
    lane = lax.broadcasted_iota(jnp.int32, (1, BLOCK), 1)
    wanted = (lax.broadcasted_iota(jnp.int32, (BLOCK, BLOCK), 0) < middle) | (
        lax.broadcasted_iota(jnp.int32, (BLOCK, BLOCK), 1) >= middle
    )
    across = [None] * col_blocks
    squares = []
    for i in range(row_blocks):
        square = summed(kept.index((i, i)))
        riding = square[middle : middle + 8]
        for n, j in enumerate((i, i + row_blocks)):
            total = jnp.where(
                lane < middle,
                riding[2 * n : 2 * n + 1],
                pltpu.roll(riding[2 * n + 1 : 2 * n + 2], middle, 1),
            )
            across[j] = jnp.broadcast_to(total, (BLOCK, BLOCK))
        squares.append(jnp.where(wanted, square, square.T))
    down = [across[i].T for i in range(row_blocks)]
    for n, (i, j) in enumerate(kept):
        centred = (squares[i] if i == j else summed(n)) - down[i] * across[j] / frame_count
        if j >= row_blocks:
            work[span(i), span(j)] = centred / math.sqrt(frame_count)
        else:
            block = centred / frame_count
            work[span(i), span(j)] = jnp.where(diagonal, block + RIDGE, block) if i == j else block

    for k in range(row_blocks):
        rest = span(k + 1, col_blocks)
        inverse = spd_inverse(work[span(k), span(k)])
        flipped = {i: work[span(k), span(i)].T for i in range(k + 1, row_blocks)}
        solved = dot32(inverse, work[span(k), rest])
        work[span(k), rest] = solved
        for i in range(k + 1, row_blocks):
            at = span(i, col_blocks)
            work[span(i), at] -= dot32(flipped[i], solved[:, (i - k - 1) * BLOCK :])
        if k:
            work[span(0, k), rest] -= dot32(work[span(0, k), span(k)], solved)
    out_ref[...] = work[:, span(row_blocks, col_blocks)]


def ridge_solve(mine, other, kept, row_blocks, col_blocks, frame_count):
    core = lax.axis_index("core").astype(jnp.int32)[None]
    return pl.pallas_call(
        functools.partial(solve_kernel, kept, row_blocks, col_blocks, float(frame_count)),
        out_shape=jax.ShapeDtypeStruct(
            (row_blocks * BLOCK, (col_blocks - row_blocks) * BLOCK), jnp.float32
        ),
        in_specs=[
            pl.BlockSpec(memory_space=pltpu.SMEM),
            pl.BlockSpec(memory_space=pltpu.VMEM),
            pl.BlockSpec(memory_space=pltpu.VMEM),
        ],
        out_specs=pl.BlockSpec(memory_space=pltpu.VMEM),
        scratch_shapes=[pltpu.VMEM((row_blocks * BLOCK, col_blocks * BLOCK), jnp.float32)],
        compiler_params=pltpu.CompilerParams(vmem_limit_bytes=VMEM),
        name="ridge_solve",
    )(core, mine, other)


def per_device(inputs, conv_weight, conv_bias, labels, rec_span):
    frames, width = inputs.shape[1:]
    feats = conv_weight.shape[2]
    label_width = labels.shape[2]
    rows = inputs[0]
    halo = jnp.concatenate(frame_halo(rows, TAP_REACH), axis=0)
    weight = conv_weight.reshape(-1, feats)
    bias = conv_bias[None]
    code = frames_code(rec_span[:, 0].reshape(2, -1, BLOCK))
    core = lax.axis_index("core").astype(jnp.int32)[None]
    row_blocks = feats // BLOCK
    col_blocks = row_blocks + label_width // BLOCK
    kept = [(i, j) for i in range(row_blocks) for j in range(i, col_blocks)]
    params = pltpu.CompilerParams(vmem_limit_bytes=VMEM)
    vmem = pl.BlockSpec(memory_space=pltpu.VMEM)
    smem = pl.BlockSpec(memory_space=pltpu.SMEM)
    anywhere = pl.BlockSpec(memory_space=pl.ANY)
    flops = 2 * frames * weight.shape[0] * feats
    joined = pl.pallas_call(
        conv_kernel,
        out_shape=jax.ShapeDtypeStruct((frames, feats + label_width), jnp.bfloat16),
        in_specs=[vmem] * 5,
        out_specs=vmem,
        scratch_shapes=[
            pltpu.VMEM((frames + 2 * PAD, width), jnp.float32),
            pltpu.VMEM((frames, weight.shape[0]), jnp.bfloat16),
        ],
        compiler_params=params,
        cost_estimate=pl.CostEstimate(flops=flops, bytes_accessed=8 << 20, transcendentals=0),
        name="conv_gelu",
    )(rows, weight, bias, labels[0], code)
    half = jax.ShapeDtypeStruct((len(kept) // 2 * BLOCK, BLOCK), jnp.float32)
    features, keep, send = pl.pallas_call(
        functools.partial(moments_kernel, kept),
        out_shape=[jax.ShapeDtypeStruct((frames, feats), jnp.bfloat16), half, half],
        in_specs=[smem] + [vmem] * 6,
        out_specs=[vmem, anywhere, anywhere],
        scratch_shapes=[
            pltpu.VMEM((frames, feats + label_width), jnp.bfloat16),
            pltpu.VMEM((2, EDGE + 2 * PAD, width), jnp.float32),
            pltpu.VMEM((2 * EDGE, weight.shape[0]), jnp.bfloat16),
            pltpu.VMEM((2,) + half.shape, jnp.float32),
            pltpu.SemaphoreType.DMA((2,)),
        ],
        compiler_params=params,
        name="moments",
    )(core, joined, rows, halo, weight, bias, code)
    mine, other = all_sum(keep, send)
    frame_count = lax.axis_size(("x", "z", "y", "core")) * inputs.shape[0] * frames
    probe_weights = ridge_solve(mine, other, kept, row_blocks, col_blocks, frame_count)
    return (features[None], probe_weights)


def solution(mesh):
    physical = Mesh(mesh.devices.reshape(4, 8, 4, 2), ("x", "z", "y", "core"))
    frame, rec = ("x", "z"), ("y", "core")
    in_specs = (P(rec, frame, None), P(), P(), P(rec, frame, None), P(None, rec, frame))
    out_specs = (P(rec, frame, None), P())
    return jax.shard_map(
        per_device, mesh=physical, in_specs=in_specs, out_specs=out_specs, check_vma=False
    )
```

```python
import functools
import math

import jax
import jax.numpy as jnp
from jax import lax
from jax.experimental import pallas as pl
from jax.experimental.pallas import tpu as pltpu
from jax.sharding import Mesh, PartitionSpec as P

RIDGE = 0.1
BLOCK = 128
GROUP = 8
TAP_REACH = 2
PAD = 8
ROWS = 256
FRONT_VMEM = 60 * 1024 * 1024
SOLVE_VMEM = 16 * 1024 * 1024


def frame_halo(rows, width):
    size = lax.axis_size(("x", "z"))
    up = [(i, i + 1) for i in range(size - 1)]
    down = [(j, i) for i, j in up]
    before = lax.ppermute(rows[-width:], ("x", "z"), up)
    after = lax.ppermute(rows[:width], ("x", "z"), down)
    return before, after


def all_sum(keep, send):
    swap = [(0, 1), (1, 0)]
    part = keep + lax.ppermute(send, "core", swap)
    peers = lax.axis_size(("x", "y"))
    rows = part.shape[0] // peers
    chunks = lax.all_to_all(
        part.reshape(peers, rows, BLOCK), ("x", "y"), split_axis=0, concat_axis=0, tiled=True
    )
    chunk = jnp.sum(chunks, axis=0)
    for bits in ((4,), (1, 2, 3)):
        chunk = chunk + sum(
            lax.ppermute(chunk, "z", [(i, i ^ bit) for i in range(lax.axis_size("z"))])
            for bit in bits
        )
    spread = jnp.broadcast_to(chunk[None], (peers, rows, BLOCK))
    full = lax.all_to_all(spread, ("x", "y"), split_axis=0, concat_axis=0, tiled=True)
    mine = full.reshape(peers * rows, BLOCK)
    other = lax.ppermute(mine, "core", swap)
    return mine, other


def gelu(value):
    return 0.5 * value * (1.0 + lax.erf(value * math.sqrt(0.5)))


def down_lanes(row):
    return jnp.broadcast_to(row, (BLOCK, BLOCK)).T


def front_kernel(
    kept, core_ref, inputs_hbm, ahead_hbm, behind_hbm, weight_hbm, bias_hbm, labels_hbm, span_hbm,
    features_hbm, keep_hbm, send_hbm, inputs, ahead, behind, weight, bias, labels, span,
    wide, taps, joined, features, halves, sems,
):
    frames, width = inputs.shape
    feats = weight.shape[1]
    loads = [
        pltpu.make_async_copy(source, target, sems.at[n])
        for n, (source, target) in enumerate(
            (
                (inputs_hbm, inputs),
                (ahead_hbm, ahead),
                (behind_hbm, behind),
                (span_hbm, span),
                (bias_hbm, bias),
                (weight_hbm, weight),
                (labels_hbm, labels),
            )
        )
    ]
    for load in loads:
        load.start()
    for load in loads[:4]:
        load.wait()
    gap = jnp.zeros((PAD - TAP_REACH, width), jnp.float32)
    wide[0:PAD, :] = jnp.concatenate([gap, ahead[...].astype(jnp.float32)], axis=0)
    wide[PAD + frames :, :] = jnp.concatenate([behind[...].astype(jnp.float32), gap], axis=0)
    wide[PAD : PAD + frames, :] = inputs[...].astype(jnp.float32)
    for start in range(0, frames, BLOCK):
        at = slice(start, start + BLOCK)
        line = slice(start // BLOCK, start // BLOCK + 1)
        spans = [
            jnp.concatenate([down_lanes(span[side, line, :].astype(jnp.float32))] * (width // BLOCK), axis=1)
            for side in (0, 1)
        ]
        for tap, offset in enumerate(range(-TAP_REACH, TAP_REACH + 1)):
            columns = slice(tap * width, (tap + 1) * width)
            if offset == 0:
                taps[at, columns] = inputs[at, :]
            else:
                shifted = wide[PAD + start + offset : PAD + start + offset + BLOCK, :]
                inside = spans[int(offset > 0)] >= abs(offset) - 0.5
                taps[at, columns] = jnp.where(inside, shifted, 0.0).astype(jnp.bfloat16)
    for load in loads[4:6]:
        load.wait()
    stores = []
    for tile, first in enumerate(range(0, frames, ROWS)):
        rows = slice(first, first + ROWS)
        pre_act = jnp.dot(taps[rows, :], weight[...], preferred_element_type=jnp.float32)
        active = gelu(pre_act + bias[...]).astype(jnp.bfloat16)
        joined[rows, :feats] = active
        features[rows, :] = active
        stores.append(
            pltpu.make_async_copy(features.at[rows], features_hbm.at[rows], sems.at[len(loads) + tile])
        )
        stores[-1].start()
    loads[6].wait()
    joined[:, feats:] = labels[...].astype(jnp.float32).astype(jnp.bfloat16)

    totals = jnp.dot(
        jnp.ones((16, frames), jnp.bfloat16), joined[...], preferred_element_type=jnp.float32
    )[0:1]
    row_blocks = feats // BLOCK
    middle = BLOCK // 2
    lane = lax.broadcasted_iota(jnp.int32, (8, BLOCK), 1)
    zero_rows = jnp.zeros((4, BLOCK), jnp.float32)
    half = len(kept) // 2
    core = core_ref[0]

    for first in range(0, row_blocks, 2):
        moments = lax.dot_general(
            joined[:, first * BLOCK : (first + 2) * BLOCK],
            joined[:, first * BLOCK :],
            (((0,), (0,)), ((), ())),
            preferred_element_type=jnp.float32,
        )
        for n, (i, j) in enumerate(kept):
            if i not in (first, first + 1):
                continue
            block = moments[
                (i - first) * BLOCK : (i - first + 1) * BLOCK,
                (j - first) * BLOCK : (j - first + 1) * BLOCK,
            ]
            if i == j:
                pair = [totals[:, m * BLOCK : (m + 1) * BLOCK] for m in (i, i + row_blocks)]
                lines = [line for t in pair for line in (t, pltpu.roll(t, middle, 1))]
                riding = jnp.where(
                    lane < middle, jnp.concatenate(lines + [zero_rows], axis=0), block[middle : middle + 8]
                )
                block = jnp.concatenate([block[:middle], riding, block[middle + 8 :]], axis=0)
            owner, place = divmod(n, half)
            halves[owner, place * BLOCK : (place + 1) * BLOCK, :] = block
    for side, target in ((core, keep_hbm), (1 - core, send_hbm)):
        stores.append(
            pltpu.make_async_copy(halves.at[side], target, sems.at[len(loads) + len(stores)])
        )
        stores[-1].start()
    for store in stores:
        store.wait()


def front(core, rows, ahead, behind, weight, bias, labels, span, kept):
    frames, width = rows.shape
    feats = weight.shape[1]
    taps = weight.shape[0]
    arrays = (rows, ahead, behind, weight, bias, labels, span)
    hbm = pl.BlockSpec(memory_space=pltpu.HBM)
    half = jax.ShapeDtypeStruct((len(kept) // 2 * BLOCK, BLOCK), jnp.float32)
    return pl.pallas_call(
        functools.partial(front_kernel, kept),
        out_shape=[jax.ShapeDtypeStruct((frames, feats), jnp.bfloat16), half, half],
        in_specs=[pl.BlockSpec(memory_space=pltpu.SMEM)] + [hbm] * len(arrays),
        out_specs=[hbm] * 3,
        scratch_shapes=[pltpu.VMEM(array.shape, array.dtype) for array in arrays]
        + [
            pltpu.VMEM((frames + 2 * PAD, width), jnp.float32),
            pltpu.VMEM((frames, taps), jnp.bfloat16),
            pltpu.VMEM((frames, feats + labels.shape[1]), jnp.bfloat16),
            pltpu.VMEM((frames, feats), jnp.bfloat16),
            pltpu.VMEM((2,) + half.shape, jnp.float32),
            pltpu.SemaphoreType.DMA((len(arrays) + frames // ROWS + 2,)),
        ],
        compiler_params=pltpu.CompilerParams(vmem_limit_bytes=FRONT_VMEM),
        name="front",
    )(core, *arrays)


def group_inverse(diag, rows):
    size = len(rows)
    for j in range(0, size, 2):
        a, b, c = diag[j][j], diag[j][j + 1], diag[j + 1][j + 1]
        scale = 1.0 / (a * c - b * b)
        left = [diag[i][j] for i in range(size)]
        right = [diag[i][j + 1] for i in range(size)]

        def solved(upper, lower):
            return (c * upper - b * lower) * scale, (a * lower - b * upper) * scale

        new = {k: solved(diag[j][k], diag[j + 1][k]) for k in range(j + 2, size)}
        for i in range(size):
            if i in (j, j + 1):
                continue
            for k in range(max(j + 2, i) if i > j else j + 2, size):
                diag[i][k] = diag[i][k] - left[i] * new[k][0] - right[i] * new[k][1]
                if i > j:
                    diag[k][i] = diag[i][k]
        for k in range(j + 2, size):
            diag[j][k], diag[j + 1][k] = new[k]
        rows[j], rows[j + 1] = solved(rows[j], rows[j + 1])
        for i in range(size):
            if i not in (j, j + 1):
                rows[i] = rows[i] - left[i] * rows[j] - right[i] * rows[j + 1]
    return rows


def spd_inverse(block):
    groups = BLOCK // GROUP
    tile = (GROUP, BLOCK)
    lane = lax.broadcasted_iota(jnp.int32, tile, 1)
    sublane = lax.broadcasted_iota(jnp.int32, tile, 0)
    part = [block[h * GROUP : (h + 1) * GROUP] for h in range(groups)]

    def spread(value):
        return jnp.broadcast_to(value, tile)

    def columns(h, first):
        return [spread(part[h][:, first + j : first + j + 1]) for j in range(GROUP)]

    def pivots(g):
        first = g * GROUP
        inside = (lane >= first) & (lane < first + GROUP)
        cols = columns(g, first)
        diag = [[None] * GROUP for _ in range(GROUP)]
        for i in range(GROUP):
            for j in range(i, GROUP):
                diag[i][j] = diag[j][i] = spread(cols[i][j : j + 1])
        rows = [
            jnp.where(
                lane == first + i, 1.0, jnp.where(inside, 0.0, spread(part[g][i : i + 1]))
            )
            for i in range(GROUP)
        ]
        return inside, diag, rows

    ahead = pivots(0)
    for g in range(groups):
        inside, diag, rows = ahead
        others = [(g + n) % groups for n in range(1, groups)]
        cols = {h: columns(h, g * GROUP) for h in others}
        rows = group_inverse(diag, rows)

        def eliminate(h):
            terms = [cols[h][j] * rows[j] for j in range(GROUP)]
            while len(terms) > 1:
                terms = [terms[n] + terms[n + 1] for n in range(0, len(terms), 2)]
            part[h] = jnp.where(inside, 0.0, part[h]) - terms[0]

        eliminate(others[0])
        if g + 1 < groups:
            ahead = pivots(g + 1)
        for h in others[1:]:
            eliminate(h)
        for i in range(GROUP):
            part[g] = jnp.where(sublane == i, rows[i], part[g])
    return jnp.concatenate(part, axis=0)


def dot32(a, b):
    return jnp.dot(a, b, precision=lax.Precision.HIGHEST, preferred_element_type=jnp.float32)


def solve_kernel(kept, row_blocks, col_blocks, frame_count, core_ref, mine_ref, other_ref, out_ref, work):
    core = core_ref[0]
    half = mine_ref.shape[0] // BLOCK

    def summed(n):
        owner, place = divmod(n, half)
        at = pl.ds(place * BLOCK, BLOCK)
        return jnp.where(core == owner, mine_ref[at, :], other_ref[at, :])

    def span(i, j=None):
        return slice(i * BLOCK, (i + 1 if j is None else j) * BLOCK)

    diagonal = lax.broadcasted_iota(jnp.int32, (BLOCK, BLOCK), 0) == lax.broadcasted_iota(
        jnp.int32, (BLOCK, BLOCK), 1
    )
    middle = BLOCK // 2
    lane = lax.broadcasted_iota(jnp.int32, (1, BLOCK), 1)
    wanted = (lax.broadcasted_iota(jnp.int32, (BLOCK, BLOCK), 0) < middle) | (
        lax.broadcasted_iota(jnp.int32, (BLOCK, BLOCK), 1) >= middle
    )
    across = [None] * col_blocks
    squares = []
    for i in range(row_blocks):
        square = summed(kept.index((i, i)))
        riding = square[middle : middle + 8]
        for n, j in enumerate((i, i + row_blocks)):
            total = jnp.where(
                lane < middle,
                riding[2 * n : 2 * n + 1],
                pltpu.roll(riding[2 * n + 1 : 2 * n + 2], middle, 1),
            )
            across[j] = jnp.broadcast_to(total, (BLOCK, BLOCK))
        squares.append(jnp.where(wanted, square, square.T))
    down = [across[i].T for i in range(row_blocks)]
    for n, (i, j) in enumerate(kept):
        centred = (squares[i] if i == j else summed(n)) - down[i] * across[j] / frame_count
        if j >= row_blocks:
            work[span(i), span(j)] = centred / math.sqrt(frame_count)
        else:
            block = centred / frame_count
            work[span(i), span(j)] = jnp.where(diagonal, block + RIDGE, block) if i == j else block

    for k in range(row_blocks):
        rest = span(k + 1, col_blocks)
        inverse = spd_inverse(work[span(k), span(k)])
        flipped = {i: work[span(k), span(i)].T for i in range(k + 1, row_blocks)}
        solved = dot32(inverse, work[span(k), rest])
        work[span(k), rest] = solved
        for i in range(k + 1, row_blocks):
            at = span(i, col_blocks)
            work[span(i), at] -= dot32(flipped[i], solved[:, (i - k - 1) * BLOCK :])
        if k:
            work[span(0, k), rest] -= dot32(work[span(0, k), span(k)], solved)
    out_ref[...] = work[:, span(row_blocks, col_blocks)]


def ridge_solve(mine, other, kept, row_blocks, col_blocks, frame_count):
    core = lax.axis_index("core").astype(jnp.int32)[None]
    return pl.pallas_call(
        functools.partial(solve_kernel, kept, row_blocks, col_blocks, float(frame_count)),
        out_shape=jax.ShapeDtypeStruct(
            (row_blocks * BLOCK, (col_blocks - row_blocks) * BLOCK), jnp.float32
        ),
        in_specs=[
            pl.BlockSpec(memory_space=pltpu.SMEM),
            pl.BlockSpec(memory_space=pltpu.VMEM),
            pl.BlockSpec(memory_space=pltpu.VMEM),
        ],
        out_specs=pl.BlockSpec(memory_space=pltpu.VMEM),
        scratch_shapes=[pltpu.VMEM((row_blocks * BLOCK, col_blocks * BLOCK), jnp.float32)],
        compiler_params=pltpu.CompilerParams(vmem_limit_bytes=SOLVE_VMEM),
        name="ridge_solve",
    )(core, mine, other)


def per_device(inputs, conv_weight, conv_bias, labels, rec_span):
    frames = inputs.shape[1]
    feats = conv_weight.shape[2]
    row_blocks = feats // BLOCK
    col_blocks = row_blocks + labels.shape[2] // BLOCK
    kept = [(i, j) for i in range(row_blocks) for j in range(i, col_blocks)]
    core = lax.axis_index("core").astype(jnp.int32)[None]
    ahead, behind = frame_halo(inputs[0], TAP_REACH)
    features, keep, send = front(
        core,
        inputs[0],
        ahead,
        behind,
        conv_weight.reshape(-1, feats),
        conv_bias[None],
        labels[0],
        rec_span[:, 0].reshape(2, -1, BLOCK),
        kept,
    )
    mine, other = all_sum(keep, send)
    frame_count = lax.axis_size(("x", "z", "y", "core")) * inputs.shape[0] * frames
    probe_weights = ridge_solve(mine, other, kept, row_blocks, col_blocks, frame_count)
    return (features[None], probe_weights)


def solution(mesh):
    physical = Mesh(mesh.devices.reshape(4, 8, 4, 2), ("x", "z", "y", "core"))
    frame, rec = ("x", "z"), ("y", "core")
    in_specs = (P(rec, frame, None), P(), P(), P(rec, frame, None), P(None, rec, frame))
    out_specs = (P(rec, frame, None), P())
    return jax.shard_map(
        per_device, mesh=physical, in_specs=in_specs, out_specs=out_specs, check_vma=False
    )
```

```python
import functools
import math

import jax
import jax.numpy as jnp
from jax import lax
from jax.experimental import pallas as pl
from jax.experimental.pallas import tpu as pltpu
from jax.sharding import Mesh, PartitionSpec as P

RIDGE = 0.1
BLOCK = 128
GROUP = 8
STRIP = 3
TAP_REACH = 2
PAD = 8
ROWS = 256
FRONT_VMEM = 60 * 1024 * 1024
SOLVE_VMEM = 16 * 1024 * 1024


def frame_halo(rows, width):
    size = lax.axis_size(("x", "z"))
    up = [(i, i + 1) for i in range(size - 1)]
    down = [(j, i) for i, j in up]
    before = lax.ppermute(rows[-width:], ("x", "z"), up)
    after = lax.ppermute(rows[:width], ("x", "z"), down)
    return before, after


def all_sum(keep, send):
    swap = [(0, 1), (1, 0)]
    part = keep + lax.ppermute(send, "core", swap)
    peers = lax.axis_size(("x", "y"))
    rows = part.shape[0] // peers
    chunks = lax.all_to_all(
        part.reshape(peers, rows, BLOCK), ("x", "y"), split_axis=0, concat_axis=0, tiled=True
    )
    chunk = jnp.sum(chunks, axis=0)
    for bits in ((4,), (1, 2, 3)):
        chunk = chunk + sum(
            lax.ppermute(chunk, "z", [(i, i ^ bit) for i in range(lax.axis_size("z"))])
            for bit in bits
        )
    spread = jnp.broadcast_to(chunk[None], (peers, rows, BLOCK))
    full = lax.all_to_all(spread, ("x", "y"), split_axis=0, concat_axis=0, tiled=True)
    mine = full.reshape(peers * rows, BLOCK)
    other = lax.ppermute(mine, "core", swap)
    return mine, other


def gelu(value):
    return 0.5 * value * (1.0 + lax.erf(value * math.sqrt(0.5)))


def down_lanes(row):
    return jnp.broadcast_to(row, (BLOCK, BLOCK)).T


def front_kernel(
    kept, core_ref, inputs_hbm, ahead_hbm, behind_hbm, weight_hbm, bias_hbm, labels_hbm, span_hbm,
    features_hbm, keep_hbm, send_hbm, inputs, ahead, behind, weight, bias, labels, span,
    wide, taps, joined, features, halves, sems,
):
    frames, width = inputs.shape
    feats = weight.shape[1]
    loads = [
        pltpu.make_async_copy(source, target, sems.at[n])
        for n, (source, target) in enumerate(
            (
                (inputs_hbm, inputs),
                (ahead_hbm, ahead),
                (behind_hbm, behind),
                (span_hbm, span),
                (bias_hbm, bias),
                (weight_hbm, weight),
                (labels_hbm, labels),
            )
        )
    ]
    for load in loads:
        load.start()
    for load in loads[:4]:
        load.wait()
    gap = jnp.zeros((PAD - TAP_REACH, width), jnp.float32)
    wide[0:PAD, :] = jnp.concatenate([gap, ahead[...].astype(jnp.float32)], axis=0)
    wide[PAD + frames :, :] = jnp.concatenate([behind[...].astype(jnp.float32), gap], axis=0)
    wide[PAD : PAD + frames, :] = inputs[...].astype(jnp.float32)
    for start in range(0, frames, BLOCK):
        at = slice(start, start + BLOCK)
        line = slice(start // BLOCK, start // BLOCK + 1)
        spans = [
            jnp.concatenate([down_lanes(span[side, line, :].astype(jnp.float32))] * (width // BLOCK), axis=1)
            for side in (0, 1)
        ]
        for tap, offset in enumerate(range(-TAP_REACH, TAP_REACH + 1)):
            columns = slice(tap * width, (tap + 1) * width)
            if offset == 0:
                taps[at, columns] = inputs[at, :]
            else:
                shifted = wide[PAD + start + offset : PAD + start + offset + BLOCK, :]
                inside = spans[int(offset > 0)] >= abs(offset) - 0.5
                taps[at, columns] = jnp.where(inside, shifted, 0.0).astype(jnp.bfloat16)
    for load in loads[4:6]:
        load.wait()
    stores = []
    for tile, first in enumerate(range(0, frames, ROWS)):
        rows = slice(first, first + ROWS)
        pre_act = jnp.dot(taps[rows, :], weight[...], preferred_element_type=jnp.float32)
        active = gelu(pre_act + bias[...]).astype(jnp.bfloat16)
        joined[rows, :feats] = active
        features[rows, :] = active
        stores.append(
            pltpu.make_async_copy(features.at[rows], features_hbm.at[rows], sems.at[len(loads) + tile])
        )
        stores[-1].start()
    loads[6].wait()
    joined[:, feats:] = labels[...].astype(jnp.float32).astype(jnp.bfloat16)

    totals = jnp.dot(
        jnp.ones((16, frames), jnp.bfloat16), joined[...], preferred_element_type=jnp.float32
    )[0:1]
    row_blocks = feats // BLOCK
    middle = BLOCK // 2
    lane = lax.broadcasted_iota(jnp.int32, (8, BLOCK), 1)
    zero_rows = jnp.zeros((4, BLOCK), jnp.float32)
    half = len(kept) // 2
    core = core_ref[0]

    for first in range(0, row_blocks, 2):
        moments = lax.dot_general(
            joined[:, first * BLOCK : (first + 2) * BLOCK],
            joined[:, first * BLOCK :],
            (((0,), (0,)), ((), ())),
            preferred_element_type=jnp.float32,
        )
        for n, (i, j) in enumerate(kept):
            if i not in (first, first + 1):
                continue
            block = moments[
                (i - first) * BLOCK : (i - first + 1) * BLOCK,
                (j - first) * BLOCK : (j - first + 1) * BLOCK,
            ]
            if i == j:
                pair = [totals[:, m * BLOCK : (m + 1) * BLOCK] for m in (i, i + row_blocks)]
                lines = [line for t in pair for line in (t, pltpu.roll(t, middle, 1))]
                riding = jnp.where(
                    lane < middle, jnp.concatenate(lines + [zero_rows], axis=0), block[middle : middle + 8]
                )
                block = jnp.concatenate([block[:middle], riding, block[middle + 8 :]], axis=0)
            owner, place = divmod(n, half)
            halves[owner, place * BLOCK : (place + 1) * BLOCK, :] = block
    for side, target in ((core, keep_hbm), (1 - core, send_hbm)):
        stores.append(
            pltpu.make_async_copy(halves.at[side], target, sems.at[len(loads) + len(stores)])
        )
        stores[-1].start()
    for store in stores:
        store.wait()


def front(core, rows, ahead, behind, weight, bias, labels, span, kept):
    frames, width = rows.shape
    feats = weight.shape[1]
    taps = weight.shape[0]
    arrays = (rows, ahead, behind, weight, bias, labels, span)
    hbm = pl.BlockSpec(memory_space=pltpu.HBM)
    half = jax.ShapeDtypeStruct((len(kept) // 2 * BLOCK, BLOCK), jnp.float32)
    return pl.pallas_call(
        functools.partial(front_kernel, kept),
        out_shape=[jax.ShapeDtypeStruct((frames, feats), jnp.bfloat16), half, half],
        in_specs=[pl.BlockSpec(memory_space=pltpu.SMEM)] + [hbm] * len(arrays),
        out_specs=[hbm] * 3,
        scratch_shapes=[pltpu.VMEM(array.shape, array.dtype) for array in arrays]
        + [
            pltpu.VMEM((frames + 2 * PAD, width), jnp.float32),
            pltpu.VMEM((frames, taps), jnp.bfloat16),
            pltpu.VMEM((frames, feats + labels.shape[1]), jnp.bfloat16),
            pltpu.VMEM((frames, feats), jnp.bfloat16),
            pltpu.VMEM((2,) + half.shape, jnp.float32),
            pltpu.SemaphoreType.DMA((len(arrays) + frames // ROWS + 2,)),
        ],
        compiler_params=pltpu.CompilerParams(vmem_limit_bytes=FRONT_VMEM),
        name="front",
    )(core, *arrays)


def group_solve(diag, rows):
    size = len(rows)
    scale = []
    lower = [[None] * size for _ in range(size)]
    for j in range(size):
        scale.append(1.0 / diag[j][j])
        for i in range(j + 1, size):
            lower[i][j] = diag[j][i] * scale[j]
        for i in range(j + 1, size):
            for k in range(i, size):
                diag[i][k] = diag[i][k] - lower[i][j] * diag[j][k]
            rows[i] = rows[i] - lower[i][j] * rows[j]
    rows = [row * s for row, s in zip(rows, scale)]
    for j in reversed(range(size)):
        for i in range(j):
            rows[i] = rows[i] - lower[j][i] * rows[j]
    return rows


def spd_inverse(block, spot, beside):
    groups = BLOCK // GROUP
    tile = (GROUP, BLOCK)
    lane = lax.broadcasted_iota(jnp.int32, tile, 1)
    sublane = lax.broadcasted_iota(jnp.int32, tile, 0)
    part = [block[h * GROUP : (h + 1) * GROUP] for h in range(groups)]

    def spread(value):
        return jnp.broadcast_to(value, tile)

    def columns(h, first):
        return [spread(part[h][:, first + j : first + j + 1]) for j in range(GROUP)]

    def pivots(g):
        first = g * GROUP
        inside = (lane >= first) & (lane < first + GROUP)
        for i, column in enumerate(columns(g, first)):
            spot[g % 2, i] = column
        diag = [
            [spread(spot[g % 2, i, j : j + 1]) if j >= i else None for j in range(GROUP)]
            for i in range(GROUP)
        ]
        rows = [
            jnp.where(
                lane == first + i, 1.0, jnp.where(inside, 0.0, spread(part[g][i : i + 1]))
            )
            for i in range(GROUP)
        ]
        return inside, diag, rows

    ahead = pivots(0)
    for g in range(groups):
        inside, diag, rows = ahead
        others = [(g + n) % groups for n in range(1, groups)]
        cols = {h: columns(h, g * GROUP) for h in others}
        rows = group_solve(diag, rows)

        def eliminate(h):
            terms = [cols[h][j] * rows[j] for j in range(GROUP)]
            while len(terms) > 1:
                terms = [terms[n] + terms[n + 1] for n in range(0, len(terms), 2)]
            part[h] = jnp.where(inside, 0.0, part[h]) - terms[0]

        eliminate(others[0])
        if g + 1 < groups:
            ahead = pivots(g + 1)
        for call in beside[g * len(beside) // groups : (g + 1) * len(beside) // groups]:
            call()
        for h in others[1:]:
            eliminate(h)
        for i in range(GROUP):
            part[g] = jnp.where(sublane == i, rows[i], part[g])
    return jnp.concatenate(part, axis=0)


def dot32(a, b):
    return jnp.dot(a, b, precision=lax.Precision.HIGHEST, preferred_element_type=jnp.float32)


def solve_kernel(
    kept, row_blocks, col_blocks, frame_count, core_ref, mine_ref, other_ref, out_ref, work, flipped, inverse, spot
):
    core = core_ref[0]
    half = mine_ref.shape[0] // BLOCK

    def summed(n):
        owner, place = divmod(n, half)
        at = pl.ds(place * BLOCK, BLOCK)
        return jnp.where(core == owner, mine_ref[at, :], other_ref[at, :])

    def span(i, j=None):
        return slice(i * BLOCK, (i + 1 if j is None else j) * BLOCK)

    row = lax.broadcasted_iota(jnp.int32, (BLOCK, BLOCK), 0)
    column = lax.broadcasted_iota(jnp.int32, (BLOCK, BLOCK), 1)
    middle = BLOCK // 2
    totals = {}

    def read_totals(i):
        riding = summed(kept.index((i, i)))[middle : middle + 8]
        for n, j in enumerate((i, i + row_blocks)):
            totals[j] = jnp.where(
                lax.broadcasted_iota(jnp.int32, (1, BLOCK), 1) < middle,
                riding[2 * n : 2 * n + 1],
                pltpu.roll(riding[2 * n + 1 : 2 * n + 2], middle, 1),
            )

    def across(j):
        return jnp.broadcast_to(totals[j], (BLOCK, BLOCK))

    downs = {}

    def build(i, j):
        block = summed(kept.index((i, j)))
        if i == j:
            block = jnp.where((row < middle) | (column >= middle), block, block.T)
        if i not in downs:
            downs[i] = across(i).T
        centred = block - downs[i] * across(j) / frame_count
        if j >= row_blocks:
            work[span(i), span(j)] = centred / math.sqrt(frame_count)
        else:
            block = centred / frame_count
            work[span(i), span(j)] = jnp.where(row == column, block + RIDGE, block) if i == j else block

    def flip(k, i):
        flipped[k % 2, span(i), :] = work[span(k), span(i)].T

    for i in range(row_blocks):
        read_totals(i)
    build(0, 0)
    beside = [functools.partial(build, i, j) for i, j in kept if j]
    beside += [functools.partial(flip, 0, i) for i in range(1, row_blocks)]

    def solve_row(k, at):
        work[span(k), at] = dot32(inverse[k % 2], work[span(k), at])

    def eliminate(i, k, at):
        left = flipped[k % 2, span(i), :] if i > k else work[span(i), span(k)]
        work[span(i), at] -= dot32(left, work[span(k), at])

    def chunks(first):
        cuts = list(range(col_blocks, first, -STRIP))[::-1]
        return [span(max(first, cut - STRIP), cut) for cut in cuts]

    for k in range(row_blocks):
        inverse[k % 2] = spd_inverse(work[span(k), span(k)], spot, beside)
        near = k + 1
        beside = []
        if near < row_blocks:
            solve_row(k, span(near))
            eliminate(near, k, span(near))
        far = min(near + 1, col_blocks) if near < row_blocks else row_blocks
        for at in chunks(far):
            beside.append(functools.partial(solve_row, k, at))
        for i in sorted((i for i in range(row_blocks) if i != k), key=lambda i: (i != near, i)):
            first = near if i < k and near < row_blocks else max(i, far)
            for at in chunks(first):
                beside.append(functools.partial(eliminate, i, k, at))
        beside += [functools.partial(flip, near, i) for i in range(near + 1, row_blocks)]
    for call in beside:
        call()
    out_ref[...] = work[:, span(row_blocks, col_blocks)]


def ridge_solve(mine, other, kept, row_blocks, col_blocks, frame_count):
    core = lax.axis_index("core").astype(jnp.int32)[None]
    vmem = pl.BlockSpec(memory_space=pltpu.VMEM)
    return pl.pallas_call(
        functools.partial(solve_kernel, kept, row_blocks, col_blocks, float(frame_count)),
        out_shape=jax.ShapeDtypeStruct(
            (row_blocks * BLOCK, (col_blocks - row_blocks) * BLOCK), jnp.float32
        ),
        in_specs=[pl.BlockSpec(memory_space=pltpu.SMEM), vmem, vmem],
        out_specs=vmem,
        scratch_shapes=[
            pltpu.VMEM((row_blocks * BLOCK, col_blocks * BLOCK), jnp.float32),
            pltpu.VMEM((2, row_blocks * BLOCK, BLOCK), jnp.float32),
            pltpu.VMEM((2, BLOCK, BLOCK), jnp.float32),
            pltpu.VMEM((2, GROUP, GROUP, BLOCK), jnp.float32),
        ],
        compiler_params=pltpu.CompilerParams(vmem_limit_bytes=SOLVE_VMEM),
        name="ridge_solve",
    )(core, mine, other)


def per_device(inputs, conv_weight, conv_bias, labels, rec_span):
    frames = inputs.shape[1]
    feats = conv_weight.shape[2]
    row_blocks = feats // BLOCK
    col_blocks = row_blocks + labels.shape[2] // BLOCK
    kept = [(i, j) for i in range(row_blocks) for j in range(i, col_blocks)]
    core = lax.axis_index("core").astype(jnp.int32)[None]
    ahead, behind = frame_halo(inputs[0], TAP_REACH)
    features, keep, send = front(
        core,
        inputs[0],
        ahead,
        behind,
        conv_weight.reshape(-1, feats),
        conv_bias[None],
        labels[0],
        rec_span[:, 0].reshape(2, -1, BLOCK),
        kept,
    )
    mine, other = all_sum(keep, send)
    frame_count = lax.axis_size(("x", "z", "y", "core")) * inputs.shape[0] * frames
    probe_weights = ridge_solve(mine, other, kept, row_blocks, col_blocks, frame_count)
    return (features[None], probe_weights)


def solution(mesh):
    physical = Mesh(mesh.devices.reshape(4, 8, 4, 2), ("x", "z", "y", "core"))
    frame, rec = ("x", "z"), ("y", "core")
    in_specs = (P(rec, frame, None), P(), P(), P(rec, frame, None), P(None, rec, frame))
    out_specs = (P(rec, frame, None), P())
    return jax.shard_map(
        per_device, mesh=physical, in_specs=in_specs, out_specs=out_specs, check_vma=False
    )
```

```python
import functools
import math

import jax
import jax.numpy as jnp
from jax import lax
from jax.experimental import pallas as pl
from jax.experimental.pallas import tpu as pltpu
from jax.sharding import Mesh, PartitionSpec as P

RIDGE = 0.1
BLOCK = 128
GROUP = 8
STRIP = 3
TAP_REACH = 2
PAD = 8
ROWS = 256
FRONT_VMEM = 28 * 1024 * 1024
SOLVE_VMEM = 16 * 1024 * 1024


def frame_halo(rows, width):
    size = lax.axis_size(("x", "z"))
    up = [(i, i + 1) for i in range(size - 1)]
    down = [(j, i) for i, j in up]
    before = lax.ppermute(rows[-width:], ("x", "z"), up)
    after = lax.ppermute(rows[:width], ("x", "z"), down)
    return before, after


def all_sum(keep, send):
    swap = [(0, 1), (1, 0)]
    part = keep + lax.ppermute(send, "core", swap)
    peers = lax.axis_size(("x", "y"))
    rows = part.shape[0] // peers
    chunks = lax.all_to_all(
        part.reshape(peers, rows, BLOCK), ("x", "y"), split_axis=0, concat_axis=0, tiled=True
    )
    chunk = jnp.sum(chunks, axis=0)
    for bits in ((4,), (1, 2, 3)):
        chunk = chunk + sum(
            lax.ppermute(chunk, "z", [(i, i ^ bit) for i in range(lax.axis_size("z"))])
            for bit in bits
        )
    spread = jnp.broadcast_to(chunk[None], (peers, rows, BLOCK))
    full = lax.all_to_all(spread, ("x", "y"), split_axis=0, concat_axis=0, tiled=True)
    mine = full.reshape(peers * rows, BLOCK)
    other = lax.ppermute(mine, "core", swap)
    return mine, other


def gelu(value):
    return 0.5 * value * (1.0 + lax.erf(value * math.sqrt(0.5)))


def down_lanes(row):
    return jnp.broadcast_to(row, (BLOCK, BLOCK)).T


def front_kernel(
    kept, core_ref, inputs_hbm, ahead_hbm, behind_hbm, weight_hbm, bias_hbm, labels_hbm, span_hbm,
    features_hbm, keep_hbm, send_hbm, inputs, ahead, behind, weight, bias, labels, span,
    wide, taps, joined, features, halves, sems,
):
    frames, width = inputs.shape
    feats = weight.shape[1]
    loads = [
        pltpu.make_async_copy(source, target, sems.at[n])
        for n, (source, target) in enumerate(
            [
                (ahead_hbm, ahead),
                (behind_hbm, behind),
                (span_hbm, span),
                (bias_hbm, bias),
            ]
            + [
                (inputs_hbm.at[first : first + ROWS], inputs.at[first : first + ROWS])
                for first in range(0, frames, ROWS)
            ]
            + [(weight_hbm, weight), (labels_hbm, labels)]
        )
    ]
    for load in loads:
        load.start()
    for load in loads[:4]:
        load.wait()
    gap = jnp.zeros((PAD - TAP_REACH, width), jnp.float32)
    wide[0:PAD, :] = jnp.concatenate([gap, ahead[...].astype(jnp.float32)], axis=0)
    wide[PAD + frames :, :] = jnp.concatenate([behind[...].astype(jnp.float32), gap], axis=0)
    ready = 0
    for start in range(0, frames, BLOCK):
        at = slice(start, start + BLOCK)
        need = min((start + BLOCK) // ROWS + 1, frames // ROWS)
        for n in range(ready, need):
            loads[4 + n].wait()
            arrived = slice(n * ROWS, (n + 1) * ROWS)
            wide[PAD + n * ROWS : PAD + (n + 1) * ROWS, :] = inputs[arrived, :].astype(jnp.float32)
        ready = need
        line = slice(start // BLOCK, start // BLOCK + 1)
        spans = [
            jnp.concatenate([down_lanes(span[side, line, :].astype(jnp.float32))] * (width // BLOCK), axis=1)
            for side in (0, 1)
        ]
        for tap, offset in enumerate(range(-TAP_REACH, TAP_REACH + 1)):
            columns = slice(tap * width, (tap + 1) * width)
            if offset == 0:
                taps[at, columns] = inputs[at, :]
            else:
                shifted = wide[PAD + start + offset : PAD + start + offset + BLOCK, :]
                inside = spans[int(offset > 0)] >= abs(offset) - 0.5
                taps[at, columns] = jnp.where(inside, shifted, 0.0).astype(jnp.bfloat16)
    loads[-2].wait()
    stores = []
    for tile, first in enumerate(range(0, frames, ROWS)):
        rows = slice(first, first + ROWS)
        pre_act = jnp.dot(taps[rows, :], weight[...], preferred_element_type=jnp.float32)
        active = gelu(pre_act + bias[...]).astype(jnp.bfloat16)
        joined[rows, :feats] = active
        features[rows, :] = active
        stores.append(
            pltpu.make_async_copy(features.at[rows], features_hbm.at[rows], sems.at[len(loads) + tile])
        )
        stores[-1].start()
    loads[-1].wait()
    joined[:, feats:] = labels[...].astype(jnp.float32).astype(jnp.bfloat16)

    totals = jnp.dot(
        jnp.ones((16, frames), jnp.bfloat16), joined[...], preferred_element_type=jnp.float32
    )[0:1]
    row_blocks = feats // BLOCK
    middle = BLOCK // 2
    lane = lax.broadcasted_iota(jnp.int32, (8, BLOCK), 1)
    zero_rows = jnp.zeros((4, BLOCK), jnp.float32)
    half = len(kept) // 2
    core = core_ref[0]

    for first in range(0, row_blocks, 2):
        moments = lax.dot_general(
            joined[:, first * BLOCK : (first + 2) * BLOCK],
            joined[:, first * BLOCK :],
            (((0,), (0,)), ((), ())),
            preferred_element_type=jnp.float32,
        )
        for n, (i, j) in enumerate(kept):
            if i not in (first, first + 1):
                continue
            block = moments[
                (i - first) * BLOCK : (i - first + 1) * BLOCK,
                (j - first) * BLOCK : (j - first + 1) * BLOCK,
            ]
            if i == j:
                pair = [totals[:, m * BLOCK : (m + 1) * BLOCK] for m in (i, i + row_blocks)]
                lines = [line for t in pair for line in (t, pltpu.roll(t, middle, 1))]
                riding = jnp.where(
                    lane < middle, jnp.concatenate(lines + [zero_rows], axis=0), block[middle : middle + 8]
                )
                block = jnp.concatenate([block[:middle], riding, block[middle + 8 :]], axis=0)
            owner, place = divmod(n, half)
            halves[owner, place * BLOCK : (place + 1) * BLOCK, :] = block
    for side, target in ((core, keep_hbm), (1 - core, send_hbm)):
        stores.append(
            pltpu.make_async_copy(halves.at[side], target, sems.at[len(loads) + len(stores)])
        )
        stores[-1].start()
    for store in stores:
        store.wait()


def front(core, rows, ahead, behind, weight, bias, labels, span, kept):
    frames, width = rows.shape
    feats = weight.shape[1]
    taps = weight.shape[0]
    rows, weight, bias, labels, span = (
        pltpu.with_memory_space_constraint(array, pltpu.HBM)
        for array in (rows, weight, bias, labels, span)
    )
    arrays = (rows, ahead, behind, weight, bias, labels, span)
    hbm = pl.BlockSpec(memory_space=pltpu.HBM)
    half = jax.ShapeDtypeStruct((len(kept) // 2 * BLOCK, BLOCK), jnp.float32)
    return pl.pallas_call(
        functools.partial(front_kernel, kept),
        out_shape=[jax.ShapeDtypeStruct((frames, feats), jnp.bfloat16), half, half],
        in_specs=[pl.BlockSpec(memory_space=pltpu.SMEM)] + [hbm] * len(arrays),
        out_specs=[hbm] * 3,
        scratch_shapes=[pltpu.VMEM(array.shape, array.dtype) for array in arrays]
        + [
            pltpu.VMEM((frames + 2 * PAD, width), jnp.float32),
            pltpu.VMEM((frames, taps), jnp.bfloat16),
            pltpu.VMEM((frames, feats + labels.shape[1]), jnp.bfloat16),
            pltpu.VMEM((frames, feats), jnp.bfloat16),
            pltpu.VMEM((2,) + half.shape, jnp.float32),
            pltpu.SemaphoreType.DMA((len(arrays) - 1 + 2 * (frames // ROWS) + 2,)),
        ],
        compiler_params=pltpu.CompilerParams(vmem_limit_bytes=FRONT_VMEM),
        name="front",
    )(core, *arrays)


def tree_sum(terms):
    while len(terms) > 1:
        terms = [terms[n] + terms[n + 1] for n in range(0, len(terms), 2)]
    return terms[0]


def group_solve(diag, rows, near):
    size = len(rows)
    scale = []
    lower = [[None] * size for _ in range(size)]
    for j in range(size):
        scale.append(1.0 / diag[j][j])
        for i in range(j + 1, size):
            lower[i][j] = diag[j][i] * scale[j]
        for i in range(j + 1, size):
            for k in range(i, size):
                diag[i][k] = diag[i][k] - lower[i][j] * diag[j][k]
            rows[i] = rows[i] - lower[i][j] * rows[j]
    rows = [row * s for row, s in zip(rows, scale)]
    for j in reversed(range(size)):
        for i in range(j):
            rows[i] = rows[i] - lower[j][i] * rows[j]
    return rows, tree_sum([column * row for column, row in zip(near, rows)])


def spd_inverse(block, spot, beside):
    groups = BLOCK // GROUP
    tile = (GROUP, BLOCK)
    lane = lax.broadcasted_iota(jnp.int32, tile, 1)
    sublane = lax.broadcasted_iota(jnp.int32, tile, 0)
    part = [block[h * GROUP : (h + 1) * GROUP] for h in range(groups)]

    def spread(value):
        return jnp.broadcast_to(value, tile)

    def columns(h, first):
        return [spread(part[h][:, first + j : first + j + 1]) for j in range(GROUP)]

    def pivots(g):
        first = g * GROUP
        inside = (lane >= first) & (lane < first + GROUP)
        for i, column in enumerate(columns(g, first)):
            spot[g % 2, i] = column
        diag = [
            [spread(spot[g % 2, i, j : j + 1]) if j >= i else None for j in range(GROUP)]
            for i in range(GROUP)
        ]
        rows = [
            jnp.where(
                lane == first + i, 1.0, jnp.where(inside, 0.0, spread(part[g][i : i + 1]))
            )
            for i in range(GROUP)
        ]
        return inside, diag, rows

    ahead = pivots(0)
    for g in range(groups):
        inside, diag, rows = ahead
        others = [(g + n) % groups for n in range(1, groups)]
        cols = {h: columns(h, g * GROUP) for h in others}
        rows, product = group_solve(diag, rows, cols[others[0]])
        part[others[0]] = jnp.where(inside, 0.0, part[others[0]]) - product
        if g + 1 < groups:
            ahead = pivots(g + 1)
        for call in beside[g * len(beside) // groups : (g + 1) * len(beside) // groups]:
            call()
        for h in others[1:]:
            product = tree_sum([column * row for column, row in zip(cols[h], rows)])
            part[h] = jnp.where(inside, 0.0, part[h]) - product
        for i in range(GROUP):
            part[g] = jnp.where(sublane == i, rows[i], part[g])
    return jnp.concatenate(part, axis=0)


def dot32(a, b):
    return jnp.dot(a, b, precision=lax.Precision.HIGHEST, preferred_element_type=jnp.float32)


def solve_kernel(
    kept, row_blocks, col_blocks, frame_count, core_ref, mine_ref, other_ref, out_hbm, work, flipped, inverse, spot, sems
):
    core = core_ref[0]
    half = mine_ref.shape[0] // BLOCK

    def summed(n):
        owner, place = divmod(n, half)
        at = pl.ds(place * BLOCK, BLOCK)
        return jnp.where(core == owner, mine_ref[at, :], other_ref[at, :])

    def span(i, j=None):
        return slice(i * BLOCK, (i + 1 if j is None else j) * BLOCK)

    row = lax.broadcasted_iota(jnp.int32, (BLOCK, BLOCK), 0)
    column = lax.broadcasted_iota(jnp.int32, (BLOCK, BLOCK), 1)
    middle = BLOCK // 2
    totals = {}

    def read_totals(i):
        riding = summed(kept.index((i, i)))[middle : middle + 8]
        for n, j in enumerate((i, i + row_blocks)):
            totals[j] = jnp.where(
                lax.broadcasted_iota(jnp.int32, (1, BLOCK), 1) < middle,
                riding[2 * n : 2 * n + 1],
                pltpu.roll(riding[2 * n + 1 : 2 * n + 2], middle, 1),
            )

    def across(j):
        return jnp.broadcast_to(totals[j], (BLOCK, BLOCK))

    downs = {}

    def build(i, j):
        block = summed(kept.index((i, j)))
        if i == j:
            block = jnp.where((row < middle) | (column >= middle), block, block.T)
        if i not in downs:
            downs[i] = across(i).T
        centred = block - downs[i] * across(j) / frame_count
        if j >= row_blocks:
            work[span(i), span(j)] = centred / math.sqrt(frame_count)
        else:
            block = centred / frame_count
            work[span(i), span(j)] = jnp.where(row == column, block + RIDGE, block) if i == j else block

    def flip(k, i):
        flipped[k % 2, span(i), :] = work[span(k), span(i)].T

    for i in range(row_blocks):
        read_totals(i)
    build(0, 0)
    beside = [functools.partial(build, i, j) for i, j in kept if j]
    beside += [functools.partial(flip, 0, i) for i in range(1, row_blocks)]

    def solve_row(k, at):
        work[span(k), at] = dot32(inverse[k % 2], work[span(k), at])

    def eliminate(i, k, at):
        left = flipped[k % 2, span(i), :] if i > k else work[span(i), span(k)]
        work[span(i), at] -= dot32(left, work[span(k), at])

    def chunks(first):
        cuts = list(range(col_blocks, first, -STRIP))[::-1]
        return [span(max(first, cut - STRIP), cut) for cut in cuts]

    for k in range(row_blocks):
        inverse[k % 2] = spd_inverse(work[span(k), span(k)], spot, beside)
        near = k + 1
        if near == row_blocks:
            break
        solve_row(k, span(near))
        eliminate(near, k, span(near))
        far = near + 1
        beside = []
        for at in chunks(far):
            beside.append(functools.partial(solve_row, k, at))
        for i in sorted((i for i in range(row_blocks) if i != k), key=lambda i: (i != near, i)):
            first = near if i < k else max(i, far)
            for at in chunks(first):
                beside.append(functools.partial(eliminate, i, k, at))
        beside += [functools.partial(flip, near, i) for i in range(near + 1, row_blocks)]
    last = row_blocks - 1
    answer = span(row_blocks, col_blocks)
    solve_row(last, answer)
    copies = []
    for i in (last, *range(last)):
        if i != last:
            eliminate(i, last, answer)
        copies.append(
            pltpu.make_async_copy(work.at[span(i), answer], out_hbm.at[span(i)], sems.at[i])
        )
        copies[-1].start()
    for copy in copies:
        copy.wait()


def ridge_solve(mine, other, kept, row_blocks, col_blocks, frame_count):
    core = lax.axis_index("core").astype(jnp.int32)[None]
    vmem = pl.BlockSpec(memory_space=pltpu.VMEM)
    return pl.pallas_call(
        functools.partial(solve_kernel, kept, row_blocks, col_blocks, float(frame_count)),
        out_shape=jax.ShapeDtypeStruct(
            (row_blocks * BLOCK, (col_blocks - row_blocks) * BLOCK), jnp.float32
        ),
        in_specs=[pl.BlockSpec(memory_space=pltpu.SMEM), vmem, vmem],
        out_specs=pl.BlockSpec(memory_space=pltpu.HBM),
        scratch_shapes=[
            pltpu.VMEM((row_blocks * BLOCK, col_blocks * BLOCK), jnp.float32),
            pltpu.VMEM((2, row_blocks * BLOCK, BLOCK), jnp.float32),
            pltpu.VMEM((2, BLOCK, BLOCK), jnp.float32),
            pltpu.VMEM((2, GROUP, GROUP, BLOCK), jnp.float32),
            pltpu.SemaphoreType.DMA((row_blocks,)),
        ],
        compiler_params=pltpu.CompilerParams(vmem_limit_bytes=SOLVE_VMEM),
        name="ridge_solve",
    )(core, mine, other)


def per_device(inputs, conv_weight, conv_bias, labels, rec_span):
    frames = inputs.shape[1]
    feats = conv_weight.shape[2]
    row_blocks = feats // BLOCK
    col_blocks = row_blocks + labels.shape[2] // BLOCK
    kept = [(i, j) for i in range(row_blocks) for j in range(i, col_blocks)]
    core = lax.axis_index("core").astype(jnp.int32)[None]
    ahead, behind = frame_halo(inputs[0], TAP_REACH)
    features, keep, send = front(
        core,
        inputs[0],
        ahead,
        behind,
        conv_weight.reshape(-1, feats),
        conv_bias[None],
        labels[0],
        rec_span[:, 0].reshape(2, -1, BLOCK),
        kept,
    )
    mine, other = all_sum(keep, send)
    frame_count = lax.axis_size(("x", "z", "y", "core")) * inputs.shape[0] * frames
    probe_weights = ridge_solve(mine, other, kept, row_blocks, col_blocks, frame_count)
    return (features[None], probe_weights)


def solution(mesh):
    physical = Mesh(mesh.devices.reshape(4, 8, 4, 2), ("x", "z", "y", "core"))
    frame, rec = ("x", "z"), ("y", "core")
    in_specs = (P(rec, frame, None), P(), P(), P(rec, frame, None), P(None, rec, frame))
    out_specs = (P(rec, frame, None), P())
    return jax.shard_map(
        per_device, mesh=physical, in_specs=in_specs, out_specs=out_specs, check_vma=False
    )
```

```python
import functools
import math

import jax
import jax.numpy as jnp
from jax import lax
from jax.experimental import pallas as pl
from jax.experimental.pallas import tpu as pltpu
from jax.sharding import Mesh, PartitionSpec as P

RIDGE = 0.1
BLOCK = 128
GROUP = 8
PANEL = 4
STRIP = 3
TAP_REACH = 2
PAD = 8
ROWS = 256
FRONT_VMEM = 28 * 1024 * 1024
SOLVE_VMEM = 16 * 1024 * 1024


def frame_halo(rows, width):
    size = lax.axis_size(("x", "z"))
    up = [(i, i + 1) for i in range(size - 1)]
    down = [(j, i) for i, j in up]
    before = lax.ppermute(rows[-width:], ("x", "z"), up)
    after = lax.ppermute(rows[:width], ("x", "z"), down)
    return before, after


def all_sum(keep, send):
    swap = [(0, 1), (1, 0)]
    part = keep + lax.ppermute(send, "core", swap)
    peers = lax.axis_size(("x", "y"))
    rows = part.shape[0] // peers
    chunks = lax.all_to_all(
        part.reshape(peers, rows, BLOCK), ("x", "y"), split_axis=0, concat_axis=0, tiled=True
    )
    chunk = jnp.sum(chunks, axis=0)
    for bits in ((4,), (1, 2, 3)):
        chunk = chunk + sum(
            lax.ppermute(chunk, "z", [(i, i ^ bit) for i in range(lax.axis_size("z"))])
            for bit in bits
        )
    spread = jnp.broadcast_to(chunk[None], (peers, rows, BLOCK))
    full = lax.all_to_all(spread, ("x", "y"), split_axis=0, concat_axis=0, tiled=True)
    mine = full.reshape(peers * rows, BLOCK)
    other = lax.ppermute(mine, "core", swap)
    return mine, other


def gelu(value):
    return 0.5 * value * (1.0 + lax.erf(value * math.sqrt(0.5)))


def down_lanes(row):
    return jnp.broadcast_to(row, (BLOCK, BLOCK)).T


def front_kernel(
    kept, core_ref, inputs_hbm, ahead_hbm, behind_hbm, weight_hbm, bias_hbm, labels_hbm, span_hbm,
    features_hbm, keep_hbm, send_hbm, inputs, ahead, behind, weight, bias, labels, span,
    wide, taps, joined, features, halves, sems,
):
    frames, width = inputs.shape
    feats = weight.shape[1]
    loads = [
        pltpu.make_async_copy(source, target, sems.at[n])
        for n, (source, target) in enumerate(
            [
                (ahead_hbm, ahead),
                (behind_hbm, behind),
                (span_hbm, span),
                (bias_hbm, bias),
            ]
            + [
                (inputs_hbm.at[first : first + ROWS], inputs.at[first : first + ROWS])
                for first in range(0, frames, ROWS)
            ]
            + [(weight_hbm, weight), (labels_hbm, labels)]
        )
    ]
    for load in loads:
        load.start()
    for load in loads[:4]:
        load.wait()
    gap = jnp.zeros((PAD - TAP_REACH, width), jnp.float32)
    wide[0:PAD, :] = jnp.concatenate([gap, ahead[...].astype(jnp.float32)], axis=0)
    wide[PAD + frames :, :] = jnp.concatenate([behind[...].astype(jnp.float32), gap], axis=0)
    ready = 0
    for start in range(0, frames, BLOCK):
        at = slice(start, start + BLOCK)
        need = min((start + BLOCK) // ROWS + 1, frames // ROWS)
        for n in range(ready, need):
            loads[4 + n].wait()
            arrived = slice(n * ROWS, (n + 1) * ROWS)
            wide[PAD + n * ROWS : PAD + (n + 1) * ROWS, :] = inputs[arrived, :].astype(jnp.float32)
        ready = need
        line = slice(start // BLOCK, start // BLOCK + 1)
        spans = [
            jnp.concatenate([down_lanes(span[side, line, :].astype(jnp.float32))] * (width // BLOCK), axis=1)
            for side in (0, 1)
        ]
        for tap, offset in enumerate(range(-TAP_REACH, TAP_REACH + 1)):
            columns = slice(tap * width, (tap + 1) * width)
            if offset == 0:
                taps[at, columns] = inputs[at, :]
            else:
                shifted = wide[PAD + start + offset : PAD + start + offset + BLOCK, :]
                inside = spans[int(offset > 0)] >= abs(offset) - 0.5
                taps[at, columns] = jnp.where(inside, shifted, 0.0).astype(jnp.bfloat16)
    loads[-2].wait()
    stores = []
    for tile, first in enumerate(range(0, frames, ROWS)):
        rows = slice(first, first + ROWS)
        pre_act = jnp.dot(taps[rows, :], weight[...], preferred_element_type=jnp.float32)
        active = gelu(pre_act + bias[...]).astype(jnp.bfloat16)
        joined[rows, :feats] = active
        features[rows, :] = active
        stores.append(
            pltpu.make_async_copy(features.at[rows], features_hbm.at[rows], sems.at[len(loads) + tile])
        )
        stores[-1].start()
    loads[-1].wait()
    joined[:, feats:] = labels[...].astype(jnp.float32).astype(jnp.bfloat16)

    totals = jnp.dot(
        jnp.ones((16, frames), jnp.bfloat16), joined[...], preferred_element_type=jnp.float32
    )[0:1]
    row_blocks = feats // BLOCK
    middle = BLOCK // 2
    lane = lax.broadcasted_iota(jnp.int32, (8, BLOCK), 1)
    zero_rows = jnp.zeros((4, BLOCK), jnp.float32)
    half = len(kept) // 2
    core = core_ref[0]

    for first in range(0, row_blocks, 2):
        moments = lax.dot_general(
            joined[:, first * BLOCK : (first + 2) * BLOCK],
            joined[:, first * BLOCK :],
            (((0,), (0,)), ((), ())),
            preferred_element_type=jnp.float32,
        )
        for n, (i, j) in enumerate(kept):
            if i not in (first, first + 1):
                continue
            block = moments[
                (i - first) * BLOCK : (i - first + 1) * BLOCK,
                (j - first) * BLOCK : (j - first + 1) * BLOCK,
            ]
            if i == j:
                pair = [totals[:, m * BLOCK : (m + 1) * BLOCK] for m in (i, i + row_blocks)]
                lines = [line for t in pair for line in (t, pltpu.roll(t, middle, 1))]
                riding = jnp.where(
                    lane < middle, jnp.concatenate(lines + [zero_rows], axis=0), block[middle : middle + 8]
                )
                block = jnp.concatenate([block[:middle], riding, block[middle + 8 :]], axis=0)
            owner, place = divmod(n, half)
            halves[owner, place * BLOCK : (place + 1) * BLOCK, :] = block
    for side, target in ((core, keep_hbm), (1 - core, send_hbm)):
        stores.append(
            pltpu.make_async_copy(halves.at[side], target, sems.at[len(loads) + len(stores)])
        )
        stores[-1].start()
    for store in stores:
        store.wait()


def front(core, rows, ahead, behind, weight, bias, labels, span, kept):
    frames, width = rows.shape
    feats = weight.shape[1]
    taps = weight.shape[0]
    rows, weight, bias, labels, span = (
        pltpu.with_memory_space_constraint(array, pltpu.HBM)
        for array in (rows, weight, bias, labels, span)
    )
    arrays = (rows, ahead, behind, weight, bias, labels, span)
    hbm = pl.BlockSpec(memory_space=pltpu.HBM)
    half = jax.ShapeDtypeStruct((len(kept) // 2 * BLOCK, BLOCK), jnp.float32)
    return pl.pallas_call(
        functools.partial(front_kernel, kept),
        out_shape=[jax.ShapeDtypeStruct((frames, feats), jnp.bfloat16), half, half],
        in_specs=[pl.BlockSpec(memory_space=pltpu.SMEM)] + [hbm] * len(arrays),
        out_specs=[hbm] * 3,
        scratch_shapes=[pltpu.VMEM(array.shape, array.dtype) for array in arrays]
        + [
            pltpu.VMEM((frames + 2 * PAD, width), jnp.float32),
            pltpu.VMEM((frames, taps), jnp.bfloat16),
            pltpu.VMEM((frames, feats + labels.shape[1]), jnp.bfloat16),
            pltpu.VMEM((frames, feats), jnp.bfloat16),
            pltpu.VMEM((2,) + half.shape, jnp.float32),
            pltpu.SemaphoreType.DMA((len(arrays) - 1 + 2 * (frames // ROWS) + 2,)),
        ],
        compiler_params=pltpu.CompilerParams(vmem_limit_bytes=FRONT_VMEM),
        name="front",
    )(core, *arrays)


def tree_sum(terms):
    while len(terms) > 1:
        terms = [terms[n] + terms[n + 1] for n in range(0, len(terms), 2)]
    return terms[0]


def group_solve(diag, rows):
    size = len(rows)
    scale = []
    lower = [[None] * size for _ in range(size)]
    for j in range(size):
        scale.append(1.0 / diag[j][j])
        for i in range(j + 1, size):
            lower[i][j] = diag[j][i] * scale[j]
        for i in range(j + 1, size):
            for k in range(i, size):
                diag[i][k] = diag[i][k] - lower[i][j] * diag[j][k]
            rows[i] = rows[i] - lower[i][j] * rows[j]
    rows = [row * s for row, s in zip(rows, scale)]
    for j in reversed(range(size)):
        for i in range(j):
            rows[i] = rows[i] - lower[j][i] * rows[j]
    return rows


def spd_inverse(block, spot, beside):
    groups = BLOCK // GROUP
    tile = (GROUP, BLOCK)
    lane = lax.broadcasted_iota(jnp.int32, tile, 1)
    sublane = lax.broadcasted_iota(jnp.int32, tile, 0)
    part = [block[h * GROUP : (h + 1) * GROUP] for h in range(groups)]

    def spread(value):
        return jnp.broadcast_to(value, tile)

    def columns(h, first):
        return [spread(part[h][:, first + j : first + j + 1]) for j in range(GROUP)]

    def pivots(g):
        first = g * GROUP
        inside = (lane >= first) & (lane < first + GROUP)
        for i, column in enumerate(columns(g, first)):
            spot[g % 2, i] = column
        diag = [
            [spread(spot[g % 2, i, j : j + 1]) if j >= i else None for j in range(GROUP)]
            for i in range(GROUP)
        ]
        rows = [
            jnp.where(
                lane == first + i, 1.0, jnp.where(inside, 0.0, spread(part[g][i : i + 1]))
            )
            for i in range(GROUP)
        ]
        return inside, diag, rows

    ahead = pivots(0)
    for g in range(groups):
        inside, diag, rows = ahead
        panel = g // PANEL
        final = (panel + 1) * PANEL >= groups
        stepped = [
            h for h in ((g + n) % groups for n in range(1, groups)) if final or 0 <= h // PANEL - panel <= 1
        ]
        cols = {h: columns(h, g * GROUP) for h in stepped}
        rows = group_solve(diag, rows)

        def eliminate(h):
            product = tree_sum([column * row for column, row in zip(cols[h], rows)])
            part[h] = jnp.where(inside, 0.0, part[h]) - product

        if g + 1 < groups:
            eliminate(stepped[0])
            ahead = pivots(g + 1)
            stepped = stepped[1:]
        for call in beside[g * len(beside) // groups : (g + 1) * len(beside) // groups]:
            call()
        for h in stepped:
            eliminate(h)
        for i in range(GROUP):
            part[g] = jnp.where(sublane == i, rows[i], part[g])
        if not final and (g + 1) % PANEL == 0:
            far = [h for h in range(groups) if not 0 <= h // PANEL - panel <= 1]
            first = panel * PANEL * GROUP
            inside = (lane >= first) & (lane < first + PANEL * GROUP)
            factor = jnp.concatenate([jnp.where(inside, part[h], 0.0) for h in far], axis=0)
            panel_rows = jnp.concatenate(
                [part[h] if h // PANEL == panel else jnp.zeros(tile, jnp.float32) for h in range(groups)],
                axis=0,
            )
            product = dot32(factor, panel_rows)
            for n, h in enumerate(far):
                part[h] = jnp.where(inside, 0.0, part[h]) - product[n * GROUP : (n + 1) * GROUP]
    return jnp.concatenate(part, axis=0)


def dot32(a, b):
    return jnp.dot(a, b, precision=lax.Precision.HIGHEST, preferred_element_type=jnp.float32)


def solve_kernel(
    kept, row_blocks, col_blocks, frame_count, core_ref, mine_ref, other_ref, out_hbm, work, flipped, inverse, spot, sems
):
    core = core_ref[0]
    half = mine_ref.shape[0] // BLOCK

    def summed(n):
        owner, place = divmod(n, half)
        at = pl.ds(place * BLOCK, BLOCK)
        return jnp.where(core == owner, mine_ref[at, :], other_ref[at, :])

    def span(i, j=None):
        return slice(i * BLOCK, (i + 1 if j is None else j) * BLOCK)

    row = lax.broadcasted_iota(jnp.int32, (BLOCK, BLOCK), 0)
    column = lax.broadcasted_iota(jnp.int32, (BLOCK, BLOCK), 1)
    middle = BLOCK // 2
    totals = {}

    def read_totals(i):
        riding = summed(kept.index((i, i)))[middle : middle + 8]
        for n, j in enumerate((i, i + row_blocks)):
            totals[j] = jnp.where(
                lax.broadcasted_iota(jnp.int32, (1, BLOCK), 1) < middle,
                riding[2 * n : 2 * n + 1],
                pltpu.roll(riding[2 * n + 1 : 2 * n + 2], middle, 1),
            )

    def across(j):
        return jnp.broadcast_to(totals[j], (BLOCK, BLOCK))

    downs = {}

    def build(i, j):
        block = summed(kept.index((i, j)))
        if i == j:
            block = jnp.where((row < middle) | (column >= middle), block, block.T)
        if i not in downs:
            downs[i] = across(i).T
        centred = block - downs[i] * across(j) / frame_count
        if j >= row_blocks:
            work[span(i), span(j)] = centred / math.sqrt(frame_count)
        else:
            block = centred / frame_count
            work[span(i), span(j)] = jnp.where(row == column, block + RIDGE, block) if i == j else block

    def flip(k, i):
        flipped[k % 2, span(i), :] = work[span(k), span(i)].T

    for i in range(row_blocks):
        read_totals(i)
    build(0, 0)
    beside = [functools.partial(build, i, j) for i, j in kept if j]
    beside += [functools.partial(flip, 0, i) for i in range(1, row_blocks)]

    def solve_row(k, at):
        work[span(k), at] = dot32(inverse[k % 2], work[span(k), at])

    def eliminate(i, k, at):
        left = flipped[k % 2, span(i), :] if i > k else work[span(i), span(k)]
        work[span(i), at] -= dot32(left, work[span(k), at])

    def chunks(first):
        cuts = list(range(col_blocks, first, -STRIP))[::-1]
        return [span(max(first, cut - STRIP), cut) for cut in cuts]

    for k in range(row_blocks):
        inverse[k % 2] = spd_inverse(work[span(k), span(k)], spot, beside)
        near = k + 1
        if near == row_blocks:
            break
        solve_row(k, span(near))
        eliminate(near, k, span(near))
        far = near + 1
        beside = []
        for at in chunks(far):
            beside.append(functools.partial(solve_row, k, at))
        for i in sorted((i for i in range(row_blocks) if i != k), key=lambda i: (i != near, i)):
            first = near if i < k else max(i, far)
            for at in chunks(first):
                beside.append(functools.partial(eliminate, i, k, at))
        beside += [functools.partial(flip, near, i) for i in range(near + 1, row_blocks)]
    last = row_blocks - 1
    answer = span(row_blocks, col_blocks)
    solve_row(last, answer)
    copies = []
    for i in (last, *range(last)):
        if i != last:
            eliminate(i, last, answer)
        copies.append(
            pltpu.make_async_copy(work.at[span(i), answer], out_hbm.at[span(i)], sems.at[i])
        )
        copies[-1].start()
    for copy in copies:
        copy.wait()


def ridge_solve(mine, other, kept, row_blocks, col_blocks, frame_count):
    core = lax.axis_index("core").astype(jnp.int32)[None]
    vmem = pl.BlockSpec(memory_space=pltpu.VMEM)
    return pl.pallas_call(
        functools.partial(solve_kernel, kept, row_blocks, col_blocks, float(frame_count)),
        out_shape=jax.ShapeDtypeStruct(
            (row_blocks * BLOCK, (col_blocks - row_blocks) * BLOCK), jnp.float32
        ),
        in_specs=[pl.BlockSpec(memory_space=pltpu.SMEM), vmem, vmem],
        out_specs=pl.BlockSpec(memory_space=pltpu.HBM),
        scratch_shapes=[
            pltpu.VMEM((row_blocks * BLOCK, col_blocks * BLOCK), jnp.float32),
            pltpu.VMEM((2, row_blocks * BLOCK, BLOCK), jnp.float32),
            pltpu.VMEM((2, BLOCK, BLOCK), jnp.float32),
            pltpu.VMEM((2, GROUP, GROUP, BLOCK), jnp.float32),
            pltpu.SemaphoreType.DMA((row_blocks,)),
        ],
        compiler_params=pltpu.CompilerParams(vmem_limit_bytes=SOLVE_VMEM),
        name="ridge_solve",
    )(core, mine, other)


def per_device(inputs, conv_weight, conv_bias, labels, rec_span):
    frames = inputs.shape[1]
    feats = conv_weight.shape[2]
    row_blocks = feats // BLOCK
    col_blocks = row_blocks + labels.shape[2] // BLOCK
    kept = [(i, j) for i in range(row_blocks) for j in range(i, col_blocks)]
    core = lax.axis_index("core").astype(jnp.int32)[None]
    ahead, behind = frame_halo(inputs[0], TAP_REACH)
    features, keep, send = front(
        core,
        inputs[0],
        ahead,
        behind,
        conv_weight.reshape(-1, feats),
        conv_bias[None],
        labels[0],
        rec_span[:, 0].reshape(2, -1, BLOCK),
        kept,
    )
    mine, other = all_sum(keep, send)
    frame_count = lax.axis_size(("x", "z", "y", "core")) * inputs.shape[0] * frames
    probe_weights = ridge_solve(mine, other, kept, row_blocks, col_blocks, frame_count)
    return (features[None], probe_weights)


def solution(mesh):
    physical = Mesh(mesh.devices.reshape(4, 8, 4, 2), ("x", "z", "y", "core"))
    frame, rec = ("x", "z"), ("y", "core")
    in_specs = (P(rec, frame, None), P(), P(), P(rec, frame, None), P(None, rec, frame))
    out_specs = (P(rec, frame, None), P())
    return jax.shard_map(
        per_device, mesh=physical, in_specs=in_specs, out_specs=out_specs, check_vma=False
    )
```

```python
import functools
import math

import jax
import jax.numpy as jnp
from jax import lax
from jax.experimental import pallas as pl
from jax.experimental.pallas import tpu as pltpu
from jax.sharding import Mesh, PartitionSpec as P

RIDGE = 0.1
BLOCK = 128
GROUP = 8
PANEL = 4
STRIP = 3
TAP_REACH = 2
PAD = 8
ROWS = 256
FRONT_VMEM = 28 * 1024 * 1024
SOLVE_VMEM = 16 * 1024 * 1024


def frame_halo(rows, width):
    size = lax.axis_size(("x", "z"))
    up = [(i, i + 1) for i in range(size - 1)]
    down = [(j, i) for i, j in up]
    before = lax.ppermute(rows[-width:], ("x", "z"), up)
    after = lax.ppermute(rows[:width], ("x", "z"), down)
    return before, after


def all_sum(keep, send):
    swap = [(0, 1), (1, 0)]
    part = keep + lax.ppermute(send, "core", swap)
    peers = lax.axis_size(("x", "y"))
    rows = part.shape[0] // peers
    chunks = lax.all_to_all(
        part.reshape(peers, rows, BLOCK), ("x", "y"), split_axis=0, concat_axis=0, tiled=True
    )
    chunk = jnp.sum(chunks, axis=0)
    for bits in ((4,), (1, 2, 3)):
        chunk = chunk + sum(
            lax.ppermute(chunk, "z", [(i, i ^ bit) for i in range(lax.axis_size("z"))])
            for bit in bits
        )
    spread = jnp.broadcast_to(chunk[None], (peers, rows, BLOCK))
    full = lax.all_to_all(spread, ("x", "y"), split_axis=0, concat_axis=0, tiled=True)
    mine = full.reshape(peers * rows, BLOCK)
    other = lax.ppermute(mine, "core", swap)
    return mine, other


def gelu(value):
    return 0.5 * value * (1.0 + lax.erf(value * math.sqrt(0.5)))


def down_lanes(row):
    return jnp.broadcast_to(row, (BLOCK, BLOCK)).T


def front_kernel(
    kept, core_ref, inputs_hbm, ahead_hbm, behind_hbm, weight_hbm, bias_hbm, labels_hbm, span_hbm,
    features_hbm, keep_hbm, send_hbm, inputs, ahead, behind, weight, bias, labels, span,
    wide, taps, joined, features, halves, sems,
):
    frames, width = inputs.shape
    feats = weight.shape[1]
    loads = [
        pltpu.make_async_copy(source, target, sems.at[n])
        for n, (source, target) in enumerate(
            [
                (ahead_hbm, ahead),
                (behind_hbm, behind),
                (span_hbm, span),
                (bias_hbm, bias),
            ]
            + [
                (inputs_hbm.at[first : first + ROWS], inputs.at[first : first + ROWS])
                for first in range(0, frames, ROWS)
            ]
            + [(weight_hbm, weight), (labels_hbm, labels)]
        )
    ]
    for load in loads:
        load.start()
    for load in loads[:4]:
        load.wait()
    gap = jnp.zeros((PAD - TAP_REACH, width), jnp.float32)
    wide[0:PAD, :] = jnp.concatenate([gap, ahead[...].astype(jnp.float32)], axis=0)
    wide[PAD + frames :, :] = jnp.concatenate([behind[...].astype(jnp.float32), gap], axis=0)
    ready = 0
    for start in range(0, frames, BLOCK):
        at = slice(start, start + BLOCK)
        need = min((start + BLOCK) // ROWS + 1, frames // ROWS)
        for n in range(ready, need):
            loads[4 + n].wait()
            arrived = slice(n * ROWS, (n + 1) * ROWS)
            wide[PAD + n * ROWS : PAD + (n + 1) * ROWS, :] = inputs[arrived, :].astype(jnp.float32)
        ready = need
        line = slice(start // BLOCK, start // BLOCK + 1)
        spans = [
            jnp.concatenate([down_lanes(span[side, line, :].astype(jnp.float32))] * (width // BLOCK), axis=1)
            for side in (0, 1)
        ]
        for tap, offset in enumerate(range(-TAP_REACH, TAP_REACH + 1)):
            columns = slice(tap * width, (tap + 1) * width)
            if offset == 0:
                taps[at, columns] = inputs[at, :]
            else:
                shifted = wide[PAD + start + offset : PAD + start + offset + BLOCK, :]
                inside = spans[int(offset > 0)] >= abs(offset) - 0.5
                taps[at, columns] = jnp.where(inside, shifted, 0.0).astype(jnp.bfloat16)
    loads[-2].wait()
    stores = []
    for tile, first in enumerate(range(0, frames, ROWS)):
        rows = slice(first, first + ROWS)
        pre_act = jnp.dot(taps[rows, :], weight[...], preferred_element_type=jnp.float32)
        active = gelu(pre_act + bias[...]).astype(jnp.bfloat16)
        joined[rows, :feats] = active
        features[rows, :] = active
        stores.append(
            pltpu.make_async_copy(features.at[rows], features_hbm.at[rows], sems.at[len(loads) + tile])
        )
        stores[-1].start()
    loads[-1].wait()
    joined[:, feats:] = labels[...].astype(jnp.float32).astype(jnp.bfloat16)

    totals = jnp.dot(
        jnp.ones((16, frames), jnp.bfloat16), joined[...], preferred_element_type=jnp.float32
    )[0:1]
    row_blocks = feats // BLOCK
    middle = BLOCK // 2
    lane = lax.broadcasted_iota(jnp.int32, (8, BLOCK), 1)
    zero_rows = jnp.zeros((4, BLOCK), jnp.float32)
    half = len(kept) // 2
    core = core_ref[0]

    for first in range(0, row_blocks, 2):
        moments = lax.dot_general(
            joined[:, first * BLOCK : (first + 2) * BLOCK],
            joined[:, first * BLOCK :],
            (((0,), (0,)), ((), ())),
            preferred_element_type=jnp.float32,
        )
        for n, (i, j) in enumerate(kept):
            if i not in (first, first + 1):
                continue
            block = moments[
                (i - first) * BLOCK : (i - first + 1) * BLOCK,
                (j - first) * BLOCK : (j - first + 1) * BLOCK,
            ]
            if i == j:
                pair = [totals[:, m * BLOCK : (m + 1) * BLOCK] for m in (i, i + row_blocks)]
                lines = [line for t in pair for line in (t, pltpu.roll(t, middle, 1))]
                riding = jnp.where(
                    lane < middle, jnp.concatenate(lines + [zero_rows], axis=0), block[middle : middle + 8]
                )
                block = jnp.concatenate([block[:middle], riding, block[middle + 8 :]], axis=0)
            owner, place = divmod(n, half)
            halves[owner, place * BLOCK : (place + 1) * BLOCK, :] = block
    for side, target in ((core, keep_hbm), (1 - core, send_hbm)):
        stores.append(
            pltpu.make_async_copy(halves.at[side], target, sems.at[len(loads) + len(stores)])
        )
        stores[-1].start()
    for store in stores:
        store.wait()


def front(core, rows, ahead, behind, weight, bias, labels, span, kept):
    frames, width = rows.shape
    feats = weight.shape[1]
    taps = weight.shape[0]
    rows, weight, bias, labels, span = (
        pltpu.with_memory_space_constraint(array, pltpu.HBM)
        for array in (rows, weight, bias, labels, span)
    )
    arrays = (rows, ahead, behind, weight, bias, labels, span)
    hbm = pl.BlockSpec(memory_space=pltpu.HBM)
    half = jax.ShapeDtypeStruct((len(kept) // 2 * BLOCK, BLOCK), jnp.float32)
    return pl.pallas_call(
        functools.partial(front_kernel, kept),
        out_shape=[jax.ShapeDtypeStruct((frames, feats), jnp.bfloat16), half, half],
        in_specs=[pl.BlockSpec(memory_space=pltpu.SMEM)] + [hbm] * len(arrays),
        out_specs=[hbm] * 3,
        scratch_shapes=[pltpu.VMEM(array.shape, array.dtype) for array in arrays]
        + [
            pltpu.VMEM((frames + 2 * PAD, width), jnp.float32),
            pltpu.VMEM((frames, taps), jnp.bfloat16),
            pltpu.VMEM((frames, feats + labels.shape[1]), jnp.bfloat16),
            pltpu.VMEM((frames, feats), jnp.bfloat16),
            pltpu.VMEM((2,) + half.shape, jnp.float32),
            pltpu.SemaphoreType.DMA((len(arrays) - 1 + 2 * (frames // ROWS) + 2,)),
        ],
        compiler_params=pltpu.CompilerParams(vmem_limit_bytes=FRONT_VMEM),
        name="front",
    )(core, *arrays)


def tree_sum(terms):
    while len(terms) > 1:
        terms = [terms[n] + terms[n + 1] for n in range(0, len(terms), 2)]
    return terms[0]


def group_solve(diag, rows, near):
    near = list(near)
    size = len(rows)
    scale = []
    lower = [[None] * size for _ in range(size)]
    for j in range(size):
        scale.append(1.0 / diag[j][j])
        for i in range(j + 1, size):
            lower[i][j] = diag[j][i] * scale[j]
        for i in range(j + 1, size):
            for k in range(i, size):
                diag[i][k] = diag[i][k] - lower[i][j] * diag[j][k]
            rows[i] = rows[i] - lower[i][j] * rows[j]
            near[i] = near[i] - lower[i][j] * near[j]
    rows = [row * s for row, s in zip(rows, scale)]
    product = tree_sum([column * row for column, row in zip(near, rows)])
    for j in reversed(range(size)):
        for i in range(j):
            rows[i] = rows[i] - lower[j][i] * rows[j]
    return rows, product


def spd_inverse(block, spot, beside):
    groups = BLOCK // GROUP
    tile = (GROUP, BLOCK)
    lane = lax.broadcasted_iota(jnp.int32, tile, 1)
    sublane = lax.broadcasted_iota(jnp.int32, tile, 0)
    part = [block[h * GROUP : (h + 1) * GROUP] for h in range(groups)]

    def spread(value):
        return jnp.broadcast_to(value, tile)

    def columns(h, first):
        return [spread(part[h][:, first + j : first + j + 1]) for j in range(GROUP)]

    def pivots(g):
        first = g * GROUP
        inside = (lane >= first) & (lane < first + GROUP)
        for i, column in enumerate(columns(g, first)):
            spot[g % 2, i] = column
        diag = [
            [spread(spot[g % 2, i, j : j + 1]) if j >= i else None for j in range(GROUP)]
            for i in range(GROUP)
        ]
        rows = [
            jnp.where(
                lane == first + i, 1.0, jnp.where(inside, 0.0, spread(part[g][i : i + 1]))
            )
            for i in range(GROUP)
        ]
        return inside, diag, rows

    ahead = pivots(0)
    for g in range(groups):
        inside, diag, rows = ahead
        panel = g // PANEL
        final = (panel + 1) * PANEL >= groups
        stepped = [
            h for h in ((g + n) % groups for n in range(1, groups)) if final or 0 <= h // PANEL - panel <= 1
        ]
        cols = {h: columns(h, g * GROUP) for h in stepped}
        rows, product = group_solve(diag, rows, cols[stepped[0]])

        def eliminate(h):
            product = tree_sum([column * row for column, row in zip(cols[h], rows)])
            part[h] = jnp.where(inside, 0.0, part[h]) - product

        if g + 1 < groups:
            part[stepped[0]] = jnp.where(inside, 0.0, part[stepped[0]]) - product
            ahead = pivots(g + 1)
            stepped = stepped[1:]
        for call in beside[g * len(beside) // groups : (g + 1) * len(beside) // groups]:
            call()
        for h in stepped:
            eliminate(h)
        for i in range(GROUP):
            part[g] = jnp.where(sublane == i, rows[i], part[g])
        if not final and (g + 1) % PANEL == 0:
            far = [h for h in range(groups) if not 0 <= h // PANEL - panel <= 1]
            first = panel * PANEL * GROUP
            inside = (lane >= first) & (lane < first + PANEL * GROUP)
            factor = jnp.concatenate([jnp.where(inside, part[h], 0.0) for h in far], axis=0)
            panel_rows = jnp.concatenate(
                [part[h] if h // PANEL == panel else jnp.zeros(tile, jnp.float32) for h in range(groups)],
                axis=0,
            )
            product = dot32(factor, panel_rows)
            for n, h in enumerate(far):
                part[h] = jnp.where(inside, 0.0, part[h]) - product[n * GROUP : (n + 1) * GROUP]
    return jnp.concatenate(part, axis=0)


def dot32(a, b):
    return jnp.dot(a, b, precision=lax.Precision.HIGHEST, preferred_element_type=jnp.float32)


def solve_kernel(
    kept, row_blocks, col_blocks, frame_count, core_ref, mine_ref, other_ref, out_hbm, work, flipped, inverse, spot, sems
):
    core = core_ref[0]
    half = mine_ref.shape[0] // BLOCK

    def summed(n):
        owner, place = divmod(n, half)
        at = pl.ds(place * BLOCK, BLOCK)
        return jnp.where(core == owner, mine_ref[at, :], other_ref[at, :])

    def span(i, j=None):
        return slice(i * BLOCK, (i + 1 if j is None else j) * BLOCK)

    row = lax.broadcasted_iota(jnp.int32, (BLOCK, BLOCK), 0)
    column = lax.broadcasted_iota(jnp.int32, (BLOCK, BLOCK), 1)
    middle = BLOCK // 2
    totals = {}

    def read_totals(i):
        riding = summed(kept.index((i, i)))[middle : middle + 8]
        for n, j in enumerate((i, i + row_blocks)):
            totals[j] = jnp.where(
                lax.broadcasted_iota(jnp.int32, (1, BLOCK), 1) < middle,
                riding[2 * n : 2 * n + 1],
                pltpu.roll(riding[2 * n + 1 : 2 * n + 2], middle, 1),
            )

    def across(j):
        return jnp.broadcast_to(totals[j], (BLOCK, BLOCK))

    downs = {}

    def build(i, j):
        block = summed(kept.index((i, j)))
        if i == j:
            block = jnp.where((row < middle) | (column >= middle), block, block.T)
        if i not in downs:
            downs[i] = across(i).T
        centred = block - downs[i] * across(j) / frame_count
        if j >= row_blocks:
            work[span(i), span(j)] = centred / math.sqrt(frame_count)
        else:
            block = centred / frame_count
            work[span(i), span(j)] = jnp.where(row == column, block + RIDGE, block) if i == j else block

    def flip(k, i):
        flipped[k % 2, span(i), :] = work[span(k), span(i)].T

    for i in range(row_blocks):
        read_totals(i)
    build(0, 0)
    beside = [functools.partial(build, i, j) for i, j in kept if j]
    beside += [functools.partial(flip, 0, i) for i in range(1, row_blocks)]

    def solve_row(k, at):
        work[span(k), at] = dot32(inverse[k % 2], work[span(k), at])

    def eliminate(i, k, at):
        left = flipped[k % 2, span(i), :] if i > k else work[span(i), span(k)]
        work[span(i), at] -= dot32(left, work[span(k), at])

    def chunks(first):
        cuts = list(range(col_blocks, first, -STRIP))[::-1]
        return [span(max(first, cut - STRIP), cut) for cut in cuts]

    for k in range(row_blocks):
        inverse[k % 2] = spd_inverse(work[span(k), span(k)], spot, beside)
        near = k + 1
        if near == row_blocks:
            break
        solve_row(k, span(near))
        eliminate(near, k, span(near))
        far = near + 1
        beside = []
        for at in chunks(far):
            beside.append(functools.partial(solve_row, k, at))
        for i in sorted((i for i in range(row_blocks) if i != k), key=lambda i: (i != near, i)):
            first = near if i < k else max(i, far)
            for at in chunks(first):
                beside.append(functools.partial(eliminate, i, k, at))
        beside += [functools.partial(flip, near, i) for i in range(near + 1, row_blocks)]
    last = row_blocks - 1
    answer = span(row_blocks, col_blocks)
    solve_row(last, answer)
    copies = []
    for i in (last, *range(last)):
        if i != last:
            eliminate(i, last, answer)
        copies.append(
            pltpu.make_async_copy(work.at[span(i), answer], out_hbm.at[span(i)], sems.at[i])
        )
        copies[-1].start()
    for copy in copies:
        copy.wait()


def ridge_solve(mine, other, kept, row_blocks, col_blocks, frame_count):
    core = lax.axis_index("core").astype(jnp.int32)[None]
    vmem = pl.BlockSpec(memory_space=pltpu.VMEM)
    return pl.pallas_call(
        functools.partial(solve_kernel, kept, row_blocks, col_blocks, float(frame_count)),
        out_shape=jax.ShapeDtypeStruct(
            (row_blocks * BLOCK, (col_blocks - row_blocks) * BLOCK), jnp.float32
        ),
        in_specs=[pl.BlockSpec(memory_space=pltpu.SMEM), vmem, vmem],
        out_specs=pl.BlockSpec(memory_space=pltpu.HBM),
        scratch_shapes=[
            pltpu.VMEM((row_blocks * BLOCK, col_blocks * BLOCK), jnp.float32),
            pltpu.VMEM((2, row_blocks * BLOCK, BLOCK), jnp.float32),
            pltpu.VMEM((2, BLOCK, BLOCK), jnp.float32),
            pltpu.VMEM((2, GROUP, GROUP, BLOCK), jnp.float32),
            pltpu.SemaphoreType.DMA((row_blocks,)),
        ],
        compiler_params=pltpu.CompilerParams(vmem_limit_bytes=SOLVE_VMEM),
        name="ridge_solve",
    )(core, mine, other)


def per_device(inputs, conv_weight, conv_bias, labels, rec_span):
    frames = inputs.shape[1]
    feats = conv_weight.shape[2]
    row_blocks = feats // BLOCK
    col_blocks = row_blocks + labels.shape[2] // BLOCK
    kept = [(i, j) for i in range(row_blocks) for j in range(i, col_blocks)]
    core = lax.axis_index("core").astype(jnp.int32)[None]
    ahead, behind = frame_halo(inputs[0], TAP_REACH)
    features, keep, send = front(
        core,
        inputs[0],
        ahead,
        behind,
        conv_weight.reshape(-1, feats),
        conv_bias[None],
        labels[0],
        rec_span[:, 0].reshape(2, -1, BLOCK),
        kept,
    )
    mine, other = all_sum(keep, send)
    frame_count = lax.axis_size(("x", "z", "y", "core")) * inputs.shape[0] * frames
    probe_weights = ridge_solve(mine, other, kept, row_blocks, col_blocks, frame_count)
    return (features[None], probe_weights)


def solution(mesh):
    physical = Mesh(mesh.devices.reshape(4, 8, 4, 2), ("x", "z", "y", "core"))
    frame, rec = ("x", "z"), ("y", "core")
    in_specs = (P(rec, frame, None), P(), P(), P(rec, frame, None), P(None, rec, frame))
    out_specs = (P(rec, frame, None), P())
    return jax.shard_map(
        per_device, mesh=physical, in_specs=in_specs, out_specs=out_specs, check_vma=False
    )
```

```python
import functools
import math

import jax
import jax.numpy as jnp
from jax import lax
from jax.experimental import pallas as pl
from jax.experimental.pallas import tpu as pltpu
from jax.sharding import Mesh, PartitionSpec as P

RIDGE = 0.1
BLOCK = 128
GROUP = 8
PANEL = 4
STRIP = 3
TAP_REACH = 2
PAD = 8
ROWS = 256
FRONT_VMEM = 28 * 1024 * 1024
SOLVE_VMEM = 16 * 1024 * 1024


def frame_halo(rows, width):
    size = lax.axis_size(("x", "z"))
    up = [(i, i + 1) for i in range(size - 1)]
    down = [(j, i) for i, j in up]
    before = lax.ppermute(rows[-width:], ("x", "z"), up)
    after = lax.ppermute(rows[:width], ("x", "z"), down)
    return before, after


def all_sum(keep, send):
    swap = [(0, 1), (1, 0)]
    part = keep + lax.ppermute(send, "core", swap)
    peers = lax.axis_size(("x", "y"))
    rows = part.shape[0] // peers
    chunks = lax.all_to_all(
        part.reshape(peers, rows, BLOCK), ("x", "y"), split_axis=0, concat_axis=0, tiled=True
    )
    chunk = jnp.sum(chunks, axis=0)
    for bits in ((4,), (1, 2, 3)):
        chunk = chunk + sum(
            lax.ppermute(chunk, "z", [(i, i ^ bit) for i in range(lax.axis_size("z"))])
            for bit in bits
        )
    spread = jnp.broadcast_to(chunk[None], (peers, rows, BLOCK))
    full = lax.all_to_all(spread, ("x", "y"), split_axis=0, concat_axis=0, tiled=True)
    mine = full.reshape(peers * rows, BLOCK)
    other = lax.ppermute(mine, "core", swap)
    return mine, other


def gelu(value):
    return 0.5 * value * (1.0 + lax.erf(value * math.sqrt(0.5)))


def down_lanes(row):
    return jnp.broadcast_to(row, (BLOCK, BLOCK)).T


def front_kernel(
    kept, core_ref, inputs_hbm, ahead_hbm, behind_hbm, weight_hbm, bias_hbm, labels_hbm, span_hbm,
    features_hbm, keep_hbm, send_hbm, inputs, ahead, behind, weight, bias, labels, span,
    wide, taps, joined, features, halves, sems,
):
    frames, width = inputs.shape
    feats = weight.shape[1]
    loads = [
        pltpu.make_async_copy(source, target, sems.at[n])
        for n, (source, target) in enumerate(
            [
                (ahead_hbm, ahead),
                (behind_hbm, behind),
                (span_hbm, span),
                (bias_hbm, bias),
            ]
            + [
                (inputs_hbm.at[first : first + ROWS], inputs.at[first : first + ROWS])
                for first in range(0, frames, ROWS)
            ]
            + [(weight_hbm, weight), (labels_hbm, labels)]
        )
    ]
    for load in loads:
        load.start()
    for load in loads[:4]:
        load.wait()
    gap = jnp.zeros((PAD - TAP_REACH, width), jnp.float32)
    wide[0:PAD, :] = jnp.concatenate([gap, ahead[...].astype(jnp.float32)], axis=0)
    wide[PAD + frames :, :] = jnp.concatenate([behind[...].astype(jnp.float32), gap], axis=0)
    ready = 0
    for start in range(0, frames, BLOCK):
        at = slice(start, start + BLOCK)
        need = min((start + BLOCK) // ROWS + 1, frames // ROWS)
        for n in range(ready, need):
            loads[4 + n].wait()
            arrived = slice(n * ROWS, (n + 1) * ROWS)
            wide[PAD + n * ROWS : PAD + (n + 1) * ROWS, :] = inputs[arrived, :].astype(jnp.float32)
        ready = need
        line = slice(start // BLOCK, start // BLOCK + 1)
        spans = [
            jnp.concatenate([down_lanes(span[side, line, :].astype(jnp.float32))] * (width // BLOCK), axis=1)
            for side in (0, 1)
        ]
        for tap, offset in enumerate(range(-TAP_REACH, TAP_REACH + 1)):
            columns = slice(tap * width, (tap + 1) * width)
            if offset == 0:
                taps[at, columns] = inputs[at, :]
            else:
                shifted = wide[PAD + start + offset : PAD + start + offset + BLOCK, :]
                inside = spans[int(offset > 0)] >= abs(offset) - 0.5
                taps[at, columns] = jnp.where(inside, shifted, 0.0).astype(jnp.bfloat16)
    loads[-2].wait()
    stores = []
    for tile, first in enumerate(range(0, frames, ROWS)):
        rows = slice(first, first + ROWS)
        pre_act = jnp.dot(taps[rows, :], weight[...], preferred_element_type=jnp.float32)
        active = gelu(pre_act + bias[...]).astype(jnp.bfloat16)
        joined[rows, :feats] = active
        features[rows, :] = active
        stores.append(
            pltpu.make_async_copy(features.at[rows], features_hbm.at[rows], sems.at[len(loads) + tile])
        )
        stores[-1].start()
    loads[-1].wait()
    joined[:, feats:] = labels[...].astype(jnp.float32).astype(jnp.bfloat16)

    totals = jnp.dot(
        jnp.ones((16, frames), jnp.bfloat16), joined[...], preferred_element_type=jnp.float32
    )[0:1]
    row_blocks = feats // BLOCK
    middle = BLOCK // 2
    lane = lax.broadcasted_iota(jnp.int32, (8, BLOCK), 1)
    zero_rows = jnp.zeros((4, BLOCK), jnp.float32)
    half = len(kept) // 2
    core = core_ref[0]

    for first in range(0, row_blocks, 2):
        moments = lax.dot_general(
            joined[:, first * BLOCK : (first + 2) * BLOCK],
            joined[:, first * BLOCK :],
            (((0,), (0,)), ((), ())),
            preferred_element_type=jnp.float32,
        )
        for n, (i, j) in enumerate(kept):
            if i not in (first, first + 1):
                continue
            block = moments[
                (i - first) * BLOCK : (i - first + 1) * BLOCK,
                (j - first) * BLOCK : (j - first + 1) * BLOCK,
            ]
            if i == j:
                pair = [totals[:, m * BLOCK : (m + 1) * BLOCK] for m in (i, i + row_blocks)]
                lines = [line for t in pair for line in (t, pltpu.roll(t, middle, 1))]
                riding = jnp.where(
                    lane < middle, jnp.concatenate(lines + [zero_rows], axis=0), block[middle : middle + 8]
                )
                block = jnp.concatenate([block[:middle], riding, block[middle + 8 :]], axis=0)
            owner, place = divmod(n, half)
            halves[owner, place * BLOCK : (place + 1) * BLOCK, :] = block
        side = first // 2
        leave = [
            pltpu.make_async_copy(halves.at[side], target, sems.at[len(loads) + len(stores)])
            for target in (keep_hbm, send_hbm)
        ]
        pl.when(core == side)(leave[0].start)
        pl.when(core != side)(leave[1].start)
        stores.append(leave[0])
    for store in stores:
        store.wait()


def front(core, rows, ahead, behind, weight, bias, labels, span, kept):
    frames, width = rows.shape
    feats = weight.shape[1]
    taps = weight.shape[0]
    rows, weight, bias, labels, span = (
        pltpu.with_memory_space_constraint(array, pltpu.HBM)
        for array in (rows, weight, bias, labels, span)
    )
    arrays = (rows, ahead, behind, weight, bias, labels, span)
    hbm = pl.BlockSpec(memory_space=pltpu.HBM)
    half = jax.ShapeDtypeStruct((len(kept) // 2 * BLOCK, BLOCK), jnp.float32)
    return pl.pallas_call(
        functools.partial(front_kernel, kept),
        out_shape=[jax.ShapeDtypeStruct((frames, feats), jnp.bfloat16), half, half],
        in_specs=[pl.BlockSpec(memory_space=pltpu.SMEM)] + [hbm] * len(arrays),
        out_specs=[hbm] * 3,
        scratch_shapes=[pltpu.VMEM(array.shape, array.dtype) for array in arrays]
        + [
            pltpu.VMEM((frames + 2 * PAD, width), jnp.float32),
            pltpu.VMEM((frames, taps), jnp.bfloat16),
            pltpu.VMEM((frames, feats + labels.shape[1]), jnp.bfloat16),
            pltpu.VMEM((frames, feats), jnp.bfloat16),
            pltpu.VMEM((2,) + half.shape, jnp.float32),
            pltpu.SemaphoreType.DMA((len(arrays) - 1 + 2 * (frames // ROWS) + 2,)),
        ],
        compiler_params=pltpu.CompilerParams(vmem_limit_bytes=FRONT_VMEM),
        name="front",
    )(core, *arrays)


def tree_sum(terms):
    while len(terms) > 1:
        terms = [terms[n] + terms[n + 1] for n in range(0, len(terms), 2)]
    return terms[0]


def group_solve(diag, rows, near):
    near = list(near)
    size = len(rows)
    scale = []
    lower = [[None] * size for _ in range(size)]
    for j in range(size):
        scale.append(1.0 / diag[j][j])
        for i in range(j + 1, size):
            lower[i][j] = diag[j][i] * scale[j]
        for i in range(j + 1, size):
            for k in range(i, size):
                diag[i][k] = diag[i][k] - lower[i][j] * diag[j][k]
            rows[i] = rows[i] - lower[i][j] * rows[j]
            near[i] = near[i] - lower[i][j] * near[j]
    rows = [row * s for row, s in zip(rows, scale)]
    product = tree_sum([column * row for column, row in zip(near, rows)])
    for j in reversed(range(size)):
        for i in range(j):
            rows[i] = rows[i] - lower[j][i] * rows[j]
    return rows, product


def spd_inverse(block, spot, beside):
    groups = BLOCK // GROUP
    tile = (GROUP, BLOCK)
    lane = lax.broadcasted_iota(jnp.int32, tile, 1)
    sublane = lax.broadcasted_iota(jnp.int32, tile, 0)
    part = [block[h * GROUP : (h + 1) * GROUP] for h in range(groups)]

    def spread(value):
        return jnp.broadcast_to(value, tile)

    def columns(h, first):
        return [spread(part[h][:, first + j : first + j + 1]) for j in range(GROUP)]

    def pivots(g):
        first = g * GROUP
        inside = (lane >= first) & (lane < first + GROUP)
        for i, column in enumerate(columns(g, first)):
            spot[g % 2, i] = column
        diag = [
            [spread(spot[g % 2, i, j : j + 1]) if j >= i else None for j in range(GROUP)]
            for i in range(GROUP)
        ]
        rows = [
            jnp.where(
                lane == first + i, 1.0, jnp.where(inside, 0.0, spread(part[g][i : i + 1]))
            )
            for i in range(GROUP)
        ]
        return inside, diag, rows

    ahead = pivots(0)
    for g in range(groups):
        inside, diag, rows = ahead
        panel = g // PANEL
        final = (panel + 1) * PANEL >= groups
        stepped = [
            h for h in ((g + n) % groups for n in range(1, groups)) if final or 0 <= h // PANEL - panel <= 1
        ]
        cols = {h: columns(h, g * GROUP) for h in stepped}
        rows, product = group_solve(diag, rows, cols[stepped[0]])

        def eliminate(h):
            product = tree_sum([column * row for column, row in zip(cols[h], rows)])
            part[h] = jnp.where(inside, 0.0, part[h]) - product

        if g + 1 < groups:
            part[stepped[0]] = jnp.where(inside, 0.0, part[stepped[0]]) - product
            ahead = pivots(g + 1)
            stepped = stepped[1:]
        for call in beside[g * len(beside) // groups : (g + 1) * len(beside) // groups]:
            call()
        for h in stepped:
            eliminate(h)
        for i in range(GROUP):
            part[g] = jnp.where(sublane == i, rows[i], part[g])
        if not final and (g + 1) % PANEL == 0:
            far = [h for h in range(groups) if not 0 <= h // PANEL - panel <= 1]
            first = panel * PANEL * GROUP
            inside = (lane >= first) & (lane < first + PANEL * GROUP)
            factor = jnp.concatenate([jnp.where(inside, part[h], 0.0) for h in far], axis=0)
            panel_rows = jnp.concatenate(
                [part[h] if h // PANEL == panel else jnp.zeros(tile, jnp.float32) for h in range(groups)],
                axis=0,
            )
            product = dot32(factor, panel_rows)
            for n, h in enumerate(far):
                part[h] = jnp.where(inside, 0.0, part[h]) - product[n * GROUP : (n + 1) * GROUP]
    return jnp.concatenate(part, axis=0)


def dot32(a, b):
    return jnp.dot(a, b, precision=lax.Precision.HIGHEST, preferred_element_type=jnp.float32)


def solve_kernel(
    kept, row_blocks, col_blocks, frame_count, core_ref, mine_ref, other_ref, out_hbm, work, flipped, inverse, spot, sems
):
    core = core_ref[0]
    half = mine_ref.shape[0] // BLOCK

    def summed(n):
        owner, place = divmod(n, half)
        at = pl.ds(place * BLOCK, BLOCK)
        return jnp.where(core == owner, mine_ref[at, :], other_ref[at, :])

    def span(i, j=None):
        return slice(i * BLOCK, (i + 1 if j is None else j) * BLOCK)

    row = lax.broadcasted_iota(jnp.int32, (BLOCK, BLOCK), 0)
    column = lax.broadcasted_iota(jnp.int32, (BLOCK, BLOCK), 1)
    middle = BLOCK // 2
    totals = {}

    def read_totals(i):
        riding = summed(kept.index((i, i)))[middle : middle + 8]
        for n, j in enumerate((i, i + row_blocks)):
            totals[j] = jnp.where(
                lax.broadcasted_iota(jnp.int32, (1, BLOCK), 1) < middle,
                riding[2 * n : 2 * n + 1],
                pltpu.roll(riding[2 * n + 1 : 2 * n + 2], middle, 1),
            )

    def across(j):
        return jnp.broadcast_to(totals[j], (BLOCK, BLOCK))

    downs = {}

    def build(i, j):
        block = summed(kept.index((i, j)))
        if i == j:
            block = jnp.where((row < middle) | (column >= middle), block, block.T)
        if i not in downs:
            downs[i] = across(i).T
        centred = block - downs[i] * across(j) / frame_count
        if j >= row_blocks:
            work[span(i), span(j)] = centred / math.sqrt(frame_count)
        else:
            block = centred / frame_count
            work[span(i), span(j)] = jnp.where(row == column, block + RIDGE, block) if i == j else block

    def flip(k, i):
        flipped[k % 2, span(i), :] = work[span(k), span(i)].T

    for i in range(row_blocks):
        read_totals(i)
    build(0, 0)
    beside = [functools.partial(build, i, j) for i, j in kept if j]
    beside += [functools.partial(flip, 0, i) for i in range(1, row_blocks)]

    def solve_row(k, at):
        work[span(k), at] = dot32(inverse[k % 2], work[span(k), at])

    def eliminate(i, k, at):
        left = flipped[k % 2, span(i), :] if i > k else work[span(i), span(k)]
        work[span(i), at] -= dot32(left, work[span(k), at])

    def chunks(first):
        cuts = list(range(col_blocks, first, -STRIP))[::-1]
        return [span(max(first, cut - STRIP), cut) for cut in cuts]

    for k in range(row_blocks):
        inverse[k % 2] = spd_inverse(work[span(k), span(k)], spot, beside)
        near = k + 1
        if near == row_blocks:
            break
        solve_row(k, span(near))
        eliminate(near, k, span(near))
        far = near + 1
        beside = []
        for at in chunks(far):
            beside.append(functools.partial(solve_row, k, at))
        for i in sorted((i for i in range(row_blocks) if i != k), key=lambda i: (i != near, i)):
            first = near if i < k else max(i, far)
            for at in chunks(first):
                beside.append(functools.partial(eliminate, i, k, at))
        beside += [functools.partial(flip, near, i) for i in range(near + 1, row_blocks)]
    last = row_blocks - 1
    answer = span(row_blocks, col_blocks)
    solve_row(last, answer)
    copies = []
    for i in (last, *range(last)):
        if i != last:
            eliminate(i, last, answer)
        copies.append(
            pltpu.make_async_copy(work.at[span(i), answer], out_hbm.at[span(i)], sems.at[i])
        )
        copies[-1].start()
    for copy in copies:
        copy.wait()


def ridge_solve(mine, other, kept, row_blocks, col_blocks, frame_count):
    core = lax.axis_index("core").astype(jnp.int32)[None]
    vmem = pl.BlockSpec(memory_space=pltpu.VMEM)
    return pl.pallas_call(
        functools.partial(solve_kernel, kept, row_blocks, col_blocks, float(frame_count)),
        out_shape=jax.ShapeDtypeStruct(
            (row_blocks * BLOCK, (col_blocks - row_blocks) * BLOCK), jnp.float32
        ),
        in_specs=[pl.BlockSpec(memory_space=pltpu.SMEM), vmem, vmem],
        out_specs=pl.BlockSpec(memory_space=pltpu.HBM),
        scratch_shapes=[
            pltpu.VMEM((row_blocks * BLOCK, col_blocks * BLOCK), jnp.float32),
            pltpu.VMEM((2, row_blocks * BLOCK, BLOCK), jnp.float32),
            pltpu.VMEM((2, BLOCK, BLOCK), jnp.float32),
            pltpu.VMEM((2, GROUP, GROUP, BLOCK), jnp.float32),
            pltpu.SemaphoreType.DMA((row_blocks,)),
        ],
        compiler_params=pltpu.CompilerParams(vmem_limit_bytes=SOLVE_VMEM),
        name="ridge_solve",
    )(core, mine, other)


def per_device(inputs, conv_weight, conv_bias, labels, rec_span):
    frames = inputs.shape[1]
    feats = conv_weight.shape[2]
    row_blocks = feats // BLOCK
    col_blocks = row_blocks + labels.shape[2] // BLOCK
    kept = [(i, j) for i in range(row_blocks) for j in range(i, col_blocks)]
    core = lax.axis_index("core").astype(jnp.int32)[None]
    ahead, behind = frame_halo(inputs[0], TAP_REACH)
    features, keep, send = front(
        core,
        inputs[0],
        ahead,
        behind,
        conv_weight.reshape(-1, feats),
        conv_bias[None],
        labels[0],
        rec_span[:, 0].reshape(2, -1, BLOCK),
        kept,
    )
    mine, other = all_sum(keep, send)
    frame_count = lax.axis_size(("x", "z", "y", "core")) * inputs.shape[0] * frames
    probe_weights = ridge_solve(mine, other, kept, row_blocks, col_blocks, frame_count)
    return (features[None], probe_weights)


def solution(mesh):
    physical = Mesh(mesh.devices.reshape(4, 8, 4, 2), ("x", "z", "y", "core"))
    frame, rec = ("x", "z"), ("y", "core")
    in_specs = (P(rec, frame, None), P(), P(), P(rec, frame, None), P(None, rec, frame))
    out_specs = (P(rec, frame, None), P())
    return jax.shard_map(
        per_device, mesh=physical, in_specs=in_specs, out_specs=out_specs, check_vma=False
    )
```
